32 devices in a mesh: dom: 8 (over y, x, core), sub: 4 (over z).
Axes of the slice: x: 2, y: 2, z: 4, core: 2. Of those that a mesh axis runs over, the one named last changes fastest.
Arguments:
- velocity: float32 [3, 40, 36, 128], P(None, 'dom', 'sub'), may hold values from -8 to 8, as said below
- displacement: float32 [3, 40, 36, 128], P(None, 'dom', 'sub'), may hold values from -0.02 to 0.02, as said below
- energy: float32 [8, 16, 16, 64], P(None, 'dom', 'sub'), may hold values from 0.5 to 2
- rho_weight: float32 [27, 16, 16, 64], P(None, 'dom', 'sub'), may hold values from 0.5 to 2
- mass_share: float32 [4, 16, 16, 64], P(None, 'dom', 'sub'), may hold values from 0.2 to 2
- energy_share: float32 [4, 16, 16, 64], P(None, 'dom', 'sub'), may hold values from 0.5 to 2
- material_id: int32 [16, 16, 64], P('dom', 'sub'), may hold values from 0 to 3
- mix_mask: int32 [4, 16, 16, 64], P(None, 'dom', 'sub'), may hold values 0 or 1
Outputs:
- accel: float32 [3, 40, 36, 128], P(None, 'dom', 'sub')
- residual: float32 [3, 40, 36, 128], P(None, 'dom', 'sub')
- energy_rate: float32 [8, 16, 16, 64], P(None, 'dom', 'sub')
The draws below stay inside these ranges and needn't reach their ends.
Inputs may be any that keep to these rules, and one draw needn't show every extreme that they name: `velocity`: every copy of a grid node holds the same value. `displacement`: every copy of a grid node holds the same value.
All inputs are finite; a program needn't handle non-finite values. No bound on the sum of `mix_mask` on one device may be relied on, other than what follows from the above.
Results may differ from the reference program's by a relative error of at most 0.0003.
Values sent between devices are 32-bit elements; how exact they have to be, the bound alone decides.
A program may use at most 64 MiB of HBM per device.

```python
import math
import jax
import jax.numpy as jnp
import numpy as np
from jax import lax

CX = 2
CY = 4
MATS = 4
EQ_ITERS = 4
CG_ITERS = 3
NX = 16
NY = 16
NZ = 64
NODE_X = 40
NODE_Y = 36
N_DOM = 8
N_SUB = 4


def spread_nodes(unique):
    along_x = jnp.arange(NODE_X, dtype=jnp.int32)
    index_x = (along_x // (2 * CX + 1) * (2 * CX) + along_x % (2 * CX + 1)) % (2 * NX)
    along_y = jnp.arange(NODE_Y, dtype=jnp.int32)
    index_y = (along_y // (2 * CY + 1) * (2 * CY) + along_y % (2 * CY + 1)) % (2 * NY)
    return jnp.take(jnp.take(unique, index_x, axis=1), index_y, axis=2)


def draw_velocity(key, part):
    extent = (3, 2 * NX, 2 * NY, 2 * NZ)
    unique = jnp.clip(jax.random.normal(key, extent, jnp.float32), -8.0, 8.0)
    return spread_nodes(unique.astype(jnp.float32)).astype(jnp.float32)


def draw_displacement(key, part):
    extent = (3, 2 * NX, 2 * NY, 2 * NZ)
    unique = jax.random.uniform(key, extent, minval=-0.02, maxval=0.02)
    return spread_nodes(unique.astype(jnp.float32)).astype(jnp.float32)


def touch_ends(values, stream_key, least, largest):
    shape = values.shape
    spot = [jax.random.randint(jax.random.fold_in(stream_key, axis), (), 0, shape[axis]) for axis in range(len(shape))]
    values = values.at[tuple(spot)].set(least)
    longest = shape.index(max(shape))
    spot[longest] = (spot[longest] + 1) % shape[longest]
    return values.at[tuple(spot)].set(largest)


def shard_levels(own_key, shape, cuts, low, top_value):
    gain, own = 1.0, jax.random.fold_in(own_key, 6)
    for dim, shards_of in cuts:
        heights = jnp.exp(jax.random.uniform(jax.random.fold_in(own, dim), (shards_of,), jnp.float32, low / len(cuts), top_value / len(cuts)))
        gain = gain * jnp.repeat(heights, shape[dim] // shards_of).reshape([-1 if axis == dim else 1 for axis in range(len(shape))])
    return gain


def setup_inputs(seed: int = 0) -> dict:
    keys = jax.random.split(jax.random.key(seed), 9)
    return {
        "velocity": draw_velocity(jax.random.fold_in(keys[8], 71), 0),
        "displacement": draw_displacement(jax.random.fold_in(keys[8], 71), 0),
        "energy": jnp.clip(jnp.exp(math.log(2.0) - 1.3862944 * jax.random.uniform(keys[2], (8, NX, NY, NZ), jnp.float32) ** shard_levels(keys[2], (8, NX, NY, NZ), ((1, 8), (2, 4)), -0.2, 0.2)), 0.5, 2.0),
        "rho_weight": jnp.clip(jnp.exp(math.log(2.0) - 1.3862944 * jax.random.uniform(keys[3], (27, NX, NY, NZ), jnp.float32) ** shard_levels(keys[3], (27, NX, NY, NZ), ((1, 8), (2, 4)), -0.2, 0.2)), 0.5, 2.0),
        "mass_share": jnp.clip(jnp.exp(math.log(2.0) - 2.3025851 * jax.random.uniform(keys[4], (MATS, NX, NY, NZ), jnp.float32) ** shard_levels(keys[4], (MATS, NX, NY, NZ), ((1, 8), (2, 4)), -0.2, 0.2)), 0.2, 2.0),
        "energy_share": jnp.clip(jnp.exp(math.log(2.0) - 1.3862944 * jax.random.uniform(keys[5], (MATS, NX, NY, NZ), jnp.float32) ** shard_levels(keys[5], (MATS, NX, NY, NZ), ((1, 8), (2, 4)), -0.2, 0.2)), 0.5, 2.0),
        "material_id": touch_ends(jax.random.randint(keys[6], (NX, NY, NZ), 0, MATS), jax.random.fold_in(keys[6], 1), 0, MATS - 1).astype(jnp.int32),
        "mix_mask": touch_ends((jax.random.randint(keys[7], (MATS, NX, NY, NZ), 0, 2) < 1).astype(jnp.int32), jax.random.fold_in(keys[7], 1), 0, 1),
    }


gammas = (1.4, 1.67, 2.0, 3.0)
cold_terms = (0.3, 1.2, 0.6, 2.4)
highest = lax.Precision.HIGHEST

def tensor_three(first, second, third):
    grid = first[:, None, None, :, None, None] * second[None, :, None, None, :, None] * third[None, None, :, None, None, :]
    rows = first.shape[0] * second.shape[0] * third.shape[0]
    columns = first.shape[1] * second.shape[1] * third.shape[1]
    return grid.reshape(rows, columns)

def basis_tables():
    spread_root = math.sqrt(0.15)
    points = np.array([0.5 - spread_root, 0.5, 0.5 + spread_root])
    quad_one = np.array([5.0, 8.0, 5.0]) / 18.0
    value_one = np.stack([2.0 * (points - 0.5) * (points - 1.0), -4.0 * points * (points - 1.0), 2.0 * points * (points - 0.5)], 1)
    slope_one = np.stack([4.0 * points - 3.0, 4.0 - 8.0 * points, 4.0 * points - 1.0], 1)
    linear_one = np.stack([1.0 - points, points], 1)
    values = tensor_three(value_one, value_one, value_one)
    slopes = np.stack([tensor_three(slope_one, value_one, value_one), tensor_three(value_one, slope_one, value_one), tensor_three(value_one, value_one, slope_one)])
    linear = tensor_three(linear_one, linear_one, linear_one)
    weights = (quad_one[:, None, None] * quad_one[None, :, None] * quad_one[None, None, :]).reshape(27)
    return (jnp.asarray(values, jnp.float32), jnp.asarray(slopes, jnp.float32), jnp.asarray(linear, jnp.float32), jnp.asarray(weights, jnp.float32))

def close_axis(array_in, axis_at):
    head_layer = lax.slice_in_dim(array_in, 0, 1, axis=axis_at)
    return jnp.concatenate([array_in, head_layer], axis_at)

def fold_periodic(array_in, axis_at):
    length = array_in.shape[axis_at] - 1
    first_layer = lax.slice_in_dim(array_in, 0, 1, axis=axis_at) + lax.slice_in_dim(array_in, length, length + 1, axis=axis_at)
    return jnp.concatenate([first_layer, lax.slice_in_dim(array_in, 1, length, axis=axis_at)], axis_at)

def zone_corners(nodes_in, zone_x, zone_y, zone_z):
    pieces = []
    for shift_x in range(3):
        for shift_y in range(3):
            for shift_z in range(3):
                pieces.append(nodes_in[:, shift_x:shift_x + 2 * zone_x:2, shift_y:shift_y + 2 * zone_y:2, shift_z:shift_z + 2 * zone_z:2])
    return jnp.stack(pieces, 0)

def weave_axis(contrib, axis_at):
    lower_part, middle_part, upper_part = (contrib[0], contrib[1], contrib[2])
    zone_count = lower_part.shape[axis_at]
    high_pad = [(0, 0)] * lower_part.ndim
    high_pad[axis_at] = (0, 1)
    low_pad = [(0, 0)] * lower_part.ndim
    low_pad[axis_at] = (1, 0)
    even_rows = jnp.pad(lower_part, high_pad) + jnp.pad(upper_part, low_pad)
    even_head = lax.slice_in_dim(even_rows, 0, zone_count, axis=axis_at)
    even_tail = lax.slice_in_dim(even_rows, zone_count, zone_count + 1, axis=axis_at)
    woven_rows = jnp.stack([even_head, middle_part], axis_at + 1)
    extent = list(even_head.shape)
    extent[axis_at] = 2 * zone_count
    return jnp.concatenate([woven_rows.reshape(extent), even_tail], axis_at)

def place_zones(contrib):
    spread = contrib.reshape((3, 3, 3) + contrib.shape[1:])
    spread = weave_axis(spread, 3)
    spread = weave_axis(spread, 3)
    return weave_axis(spread, 3)

def adjugate_of(matrix):
    cofactors = []
    for column in range(3):
        entries = []
        for line_at in range(3):
            entries.append(matrix[(line_at + 1) % 3, (column + 1) % 3] * matrix[(line_at + 2) % 3, (column + 2) % 3] - matrix[(line_at + 1) % 3, (column + 2) % 3] * matrix[(line_at + 2) % 3, (column + 1) % 3])
        cofactors.append(jnp.stack(entries))
    return jnp.stack(cofactors)

def zone_force(disp_closed, vel_closed, energy, rho_weight, mass_share, energy_share, material_id, mix_mask, tables):
    value_table, slope_table, linear_table, weight_table = tables
    zone_x, zone_y, zone_z = (energy.shape[1], energy.shape[2], energy.shape[3])
    disp_zone = zone_corners(disp_closed, zone_x, zone_y, zone_z)
    vel_zone = zone_corners(vel_closed, zone_x, zone_y, zone_z)
    identity = jnp.eye(3, dtype=jnp.float32)[:, :, None, None, None, None]
    jacobian = jnp.einsum('dqn,ncxyz->cdqxyz', slope_table, disp_zone, precision=highest) + identity
    velgrad = jnp.einsum('dqn,ncxyz->cdqxyz', slope_table, vel_zone, precision=highest)
    adjugate = adjugate_of(jacobian)
    determinant = lax.optimization_barrier(jnp.sum(jacobian[0] * adjugate[:, 0], axis=0))
    density = rho_weight / determinant
    energy_points = jnp.einsum('qj,jxyz->qxyz', linear_table, energy, precision=highest)
    material = jnp.arange(MATS, dtype=jnp.int32)[:, None, None, None]
    present = jnp.where((mix_mask == 1) | (material_id[None] == material), 1.0, 0.0).astype(jnp.float32)
    weighted = present * mass_share
    mass_fraction = weighted / lax.optimization_barrier(jnp.sum(weighted, 0, keepdims=True))
    gamma_less = jnp.asarray(gammas, jnp.float32)[:, None, None, None, None] - 1.0
    cold_part = jnp.asarray(cold_terms, jnp.float32)[:, None, None, None, None]
    pressure_load = gamma_less * density[None] * (mass_fraction * energy_share)[:, None] * energy_points[None]
    fraction = jnp.broadcast_to((present / lax.optimization_barrier(jnp.sum(present, 0, keepdims=True)))[:, None], pressure_load.shape)
    for sweep_at in range(EQ_ITERS):
        grown_part = jnp.sqrt(fraction * (pressure_load + cold_part * fraction))
        fraction = grown_part / lax.optimization_barrier(jnp.sum(grown_part, 0, keepdims=True))
    pressure = lax.optimization_barrier(jnp.sum(pressure_load + cold_part * fraction, 0))
    stress = weight_table[:, None, None, None] * pressure
    force_zone = jnp.einsum('dqn,dcqxyz->ncxyz', slope_table, adjugate * stress[None, None], precision=highest)
    divergence = lax.optimization_barrier(jnp.sum(velgrad * jnp.swapaxes(adjugate, 0, 1), (0, 1)))
    work_rate = jnp.einsum('qj,qxyz->jxyz', linear_table, stress * divergence, precision=highest)
    lumped = jnp.einsum('qj,qxyz->jxyz', linear_table, weight_table[:, None, None, None] * rho_weight, precision=highest)
    return (force_zone, -work_rate / lumped)

def mass_zone(nodes_closed, mass_weight, tables):
    value_table = tables[0]
    corners = zone_corners(nodes_closed, mass_weight.shape[1], mass_weight.shape[2], mass_weight.shape[3])
    at_points = jnp.einsum('qn,ncxyz->cqxyz', value_table, corners, precision=highest) * mass_weight[None]
    return jnp.einsum('qn,cqxyz->ncxyz', value_table, at_points, precision=highest)

def compress(copies):
    components = copies.shape[0]
    blocks = copies.reshape(components, N_DOM, 2 * CX + 1, N_SUB, 2 * CY + 1, copies.shape[3])
    return blocks[:, :, :2 * CX, :, :2 * CY].reshape(components, 2 * NX, 2 * NY, copies.shape[3])

def expand(unique):
    along_x = jnp.arange(NODE_X, dtype=jnp.int32)
    index_x = (along_x // (2 * CX + 1) * (2 * CX) + along_x % (2 * CX + 1)) % (2 * NX)
    along_y = jnp.arange(NODE_Y, dtype=jnp.int32)
    index_y = (along_y // (2 * CY + 1) * (2 * CY) + along_y % (2 * CY + 1)) % (2 * NY)
    return jnp.take(jnp.take(unique, index_x, axis=1), index_y, axis=2)

def close_all(unique):
    return close_axis(close_axis(close_axis(unique, 1), 2), 3)

def node_slab(array_in, block_at):
    return lax.dynamic_slice_in_dim(array_in, block_at * (2 * CX), 2 * CX + 1, axis=1)

def zone_slab(array_in, block_at):
    return lax.dynamic_slice_in_dim(array_in, block_at * CX, CX, axis=array_in.ndim - 3)

def finish(contrib):
    return fold_periodic(fold_periodic(place_zones(contrib), 2), 3)

def join_blocks(placed):
    main_part = placed[:, :, :2 * CX]
    tail_part = jnp.roll(placed[:, :, 2 * CX], 1, axis=0)
    main_part = main_part.at[:, :, 0].add(tail_part)
    return jnp.moveaxis(main_part, 0, 1).reshape(3, 2 * NX, 2 * NY, 2 * NZ)

def reference(velocity, displacement, energy, rho_weight, mass_share, energy_share, material_id, mix_mask):
    tables = basis_tables()
    vel_closed = close_all(compress(velocity))
    disp_closed = close_all(compress(displacement))
    mass_weight = tables[3][:, None, None, None] * rho_weight
    block_ids = jnp.arange(N_DOM, dtype=jnp.int32)

    def force_block(block_at):
        force_zone, rate_block = zone_force(node_slab(disp_closed, block_at), node_slab(vel_closed, block_at), zone_slab(energy, block_at), zone_slab(rho_weight, block_at), zone_slab(mass_share, block_at), zone_slab(energy_share, block_at), zone_slab(material_id, block_at), zone_slab(mix_mask, block_at), tables)
        return (finish(force_zone), rate_block)
    placed, rate_blocks = lax.map(force_block, block_ids)
    force_total = join_blocks(placed)
    energy_rate = jnp.moveaxis(rate_blocks, 0, 1).reshape(8, NX, NY, NZ)

    def apply_mass(node_field):
        closed = close_all(node_field)

        def mass_block(block_at):
            return finish(mass_zone(node_slab(closed, block_at), zone_slab(mass_weight, block_at), tables))
        return join_blocks(lax.map(mass_block, block_ids))
    solution = jnp.zeros_like(force_total)
    residual = force_total
    direction = force_total
    norm_now = jnp.sum(residual * residual)
    for sweep_at in range(CG_ITERS):
        mapped = apply_mass(direction)
        step_size = norm_now / jnp.sum(direction * mapped)
        solution = solution + step_size * direction
        residual = residual - step_size * mapped
        norm_next = jnp.sum(residual * residual)
        direction = residual + norm_next / norm_now * direction
        norm_now = norm_next
    return (expand(solution), expand(residual), energy_rate)
```

```python
import functools
import math

import jax
import jax.numpy as jnp
import numpy as np
from jax import lax
from jax.experimental import pallas as pl
from jax.experimental.pallas import tpu as pltpu
from jax.sharding import PartitionSpec as P
import ml_dtypes

MESH = pl.DeviceIdType.MESH
MATS = 4
EQ_ITERS = 4
CG_ITERS = 3
ROUNDS = CG_ITERS + 1

gammas = (1.4, 1.67, 2.0, 3.0)
cold_terms = (0.3, 1.2, 0.6, 2.4)

spread_root = math.sqrt(0.15)
points = np.array([0.5 - spread_root, 0.5, 0.5 + spread_root])
quad_one = np.array([5.0, 8.0, 5.0]) / 18.0
value_one = np.stack(
    [
        2.0 * (points - 0.5) * (points - 1.0),
        -4.0 * points * (points - 1.0),
        2.0 * points * (points - 0.5),
    ],
    1,
)
slope_one = np.stack([4.0 * points - 3.0, 4.0 - 8.0 * points, 4.0 * points - 1.0], 1)
linear_one = np.stack([1.0 - points, points], 1)


def round_up(value, step):
    return -(-value // step) * step


def split_table(table, axis):
    table = table.astype(np.float32)
    high = table.astype(ml_dtypes.bfloat16)
    low = (table - high.astype(np.float32)).astype(ml_dtypes.bfloat16)
    return np.concatenate([high, high, low], axis)


def depth_matrix(one, zone_z, lanes):
    table = np.zeros((2 * zone_z, lanes))
    for q in range(3):
        for z in range(zone_z):
            for k in range(3):
                table[(2 * z + k) % (2 * zone_z), q * zone_z + z] += one[q, k]
    return table


def plane_matrix(one_x, one_y, zone_x, zone_y, pad_y):
    table = np.zeros((9 * zone_x * zone_y, (2 * zone_x + 1) * pad_y))
    for a in range(3):
        for b in range(3):
            for x in range(zone_x):
                for y in range(zone_y):
                    row = ((a * 3 + b) * zone_x + x) * zone_y + y
                    for i in range(3):
                        for j in range(3):
                            table[row, (2 * x + i) * pad_y + 2 * y + j] = one_x[a, i] * one_y[b, j]
    return table


def with_faces(table, zone_x, zone_y, pad_y, pad_x):
    rows = table.T
    faces = np.zeros((2, pad_x, rows.shape[1]))
    for x in range(2 * zone_x + 1):
        faces[0, x] = rows[x * pad_y]
        faces[1, x] = rows[x * pad_y + 2 * zone_y]
    return np.concatenate([rows, faces[0], faces[1]], 0)


def split_lanes(x):
    high = x.astype(jnp.bfloat16)
    low = (x - high.astype(jnp.float32)).astype(jnp.bfloat16)
    return jnp.concatenate([high, low, high], axis=1)


def split_rows(x):
    high = x.astype(jnp.bfloat16).astype(jnp.float32)
    return jnp.concatenate([high, x - high, high], axis=0).astype(jnp.bfloat16)


def product(left, right):
    return jnp.dot(left, right, preferred_element_type=jnp.float32)


def lanes_of(x, rows):
    return jnp.concatenate([x[c * rows : (c + 1) * rows] for c in range(3)], axis=1)


def rows_of(x, lanes):
    return jnp.concatenate([x[:, c * lanes : (c + 1) * lanes] for c in range(3)], axis=0)


def kernel(
    dims,
    velocity,
    displacement,
    energy,
    rho_weight,
    mass_share,
    energy_share,
    material_id,
    mix_mask,
    depth_value,
    depth_slope,
    depth_value_t,
    depth_both_t,
    plane_value,
    plane_slopes,
    plane_value_t,
    plane_slopes_t,
    weight_table,
    accel,
    residual,
    energy_rate,
    field,
    rho,
    zone_in,
    jac,
    stress,
    part,
    total,
    face_x,
    face_y,
    corner,
    dom_parts,
    sub_parts,
    halo_send,
    halo_recv,
    dom_send,
    dom_recv,
    sub_send,
    sub_recv,
):
    n_dom, n_sub, zone_x, zone_y, zone_z, pad_x, pad_y, lanes = dims
    node_x, node_y = 2 * zone_x + 1, 2 * zone_y + 1
    plane = node_x * pad_y
    tile = zone_x * zone_y
    wide = 9 * tile
    me_dom, me_sub = lax.axis_index("dom"), lax.axis_index("sub")

    def at(shift_dom, shift_sub):
        return (lax.rem(me_dom + shift_dom + n_dom, n_dom), lax.rem(me_sub + shift_sub + n_sub, n_sub))

    corners = [(-1, -1), (-1, 1), (1, -1), (1, 1)]
    others = [at(k, 0) for k in range(1, n_dom)] + [at(0, k) for k in range(1, n_sub)]
    others += [at(dx, dy) for dx, dy in corners]
    barrier = pltpu.get_barrier_semaphore()
    for other in others:
        pl.semaphore_signal(barrier, inc=1, device_id=other, device_id_type=MESH)

    field[...] = jnp.zeros_like(field)
    for x in range(node_x):
        field[0, :, x * pad_y : x * pad_y + node_y, :] = displacement[:, x]
        field[1, :, x * pad_y : x * pad_y + node_y, :] = velocity[:, x]
    for t in range(9):
        for q in range(4):
            for x in range(zone_x):
                rho[t * tile + x * zone_y : t * tile + (x + 1) * zone_y, q * zone_z : (q + 1) * zone_z] = (
                    rho_weight[3 * t + q % 3, x]
                )
    for half in range(2):
        cols = slice(half * zone_z, (half + 1) * zone_z)
        for x in range(zone_x):
            rows = slice(x * zone_y, (x + 1) * zone_y)
            for m in range(MATS):
                present = jnp.where((mix_mask[m, x] == 1) | (material_id[x] == m), 1.0, 0.0)
                zone_in[m, rows, cols] = present
                zone_in[MATS + m, rows, cols] = mass_share[m, x]
                zone_in[2 * MATS + m, rows, cols] = energy_share[m, x]
            for j in range(8):
                zone_in[3 * MATS + j, rows, cols] = energy[j, x]

    def gradients(which):
        source = split_lanes(field[which].reshape(3 * plane, 2 * zone_z))
        by_value = split_rows(lanes_of(product(source, depth_value[...]), plane))
        by_slope = split_rows(lanes_of(product(source, depth_slope[...]), plane))
        along_xy = product(plane_slopes[...], by_value)
        along_z = product(plane_value[...], by_slope)
        jac[0] = along_xy[:wide]
        jac[1] = along_xy[wide:]
        jac[2] = along_z

    gradients(0)

    present = [zone_in[m] for m in range(MATS)]
    weighted = [present[m] * zone_in[MATS + m] for m in range(MATS)]
    weighted_sum = 1.0 / (weighted[0] + weighted[1] + weighted[2] + weighted[3])
    present_sum = 1.0 / (present[0] + present[1] + present[2] + present[3])

    def spread(x):
        return jnp.concatenate([jnp.concatenate([x, x], axis=1)] * 3, axis=0)

    start = [spread(present[m] * present_sum) for m in range(MATS)]
    load = [
        spread((gammas[m] - 1.0) * (weighted[m] * weighted_sum) * zone_in[2 * MATS + m])
        for m in range(MATS)
    ]
    lane_at = lax.broadcasted_iota(jnp.int32, (tile, lanes), 1) // zone_z
    upper = jnp.where(lane_at == 1, points[1], jnp.where(lane_at == 2, points[2], points[0])).astype(
        jnp.float32
    )
    along = []
    for j in range(4):
        low, high = zone_in[3 * MATS + 2 * j], zone_in[3 * MATS + 2 * j + 1]
        low, high = jnp.concatenate([low, low], axis=1), jnp.concatenate([high, high], axis=1)
        along.append(low + upper * (high - low))

    for a in range(3):
        rows = slice(a * 3 * tile, (a + 1) * 3 * tile)
        x_low = [linear_one[a, 0] * along[jy] + linear_one[a, 1] * along[2 + jy] for jy in range(2)]
        energy_points = jnp.concatenate(
            [linear_one[b, 0] * x_low[0] + linear_one[b, 1] * x_low[1] for b in range(3)], axis=0
        )

        def entry(c, d):
            value = jac[d, rows, c * lanes : (c + 1) * lanes]
            return value + 1.0 if c == d else value

        matrix = [[entry(c, d) for d in range(3)] for c in range(3)]
        adjugate = [[None] * 3 for _ in range(3)]
        for d in range(3):
            for c in range(3):
                adjugate[d][c] = (
                    matrix[(c + 1) % 3][(d + 1) % 3] * matrix[(c + 2) % 3][(d + 2) % 3]
                    - matrix[(c + 1) % 3][(d + 2) % 3] * matrix[(c + 2) % 3][(d + 1) % 3]
                )
        determinant = (
            matrix[0][0] * adjugate[0][0]
            + matrix[0][1] * adjugate[1][0]
            + matrix[0][2] * adjugate[2][0]
        )
        base = rho[rows, :] / determinant * energy_points
        pressure_load = [load[m] * base for m in range(MATS)]
        fraction = list(start)
        for sweep in range(EQ_ITERS):
            grown = []
            for m in range(MATS):
                square = fraction[m] * (pressure_load[m] + cold_terms[m] * fraction[m])
                grown.append(square * lax.rsqrt(jnp.maximum(square, 1e-30)))
            scale = 1.0 / ((grown[0] + grown[1]) + (grown[2] + grown[3]))
            fraction = [grown[m] * scale for m in range(MATS)]
        pressure = (
            (pressure_load[0] + cold_terms[0] * fraction[0])
            + (pressure_load[1] + cold_terms[1] * fraction[1])
            + (pressure_load[2] + cold_terms[2] * fraction[2])
            + (pressure_load[3] + cold_terms[3] * fraction[3])
        )
        weighted_pressure = weight_table[rows, :] * pressure
        for d in range(3):
            for c in range(3):
                stress[d, rows, c * lanes : (c + 1) * lanes] = weighted_pressure * adjugate[d][c]

    sends = []

    def send(source, target, to, send_sem, recv_sem):
        copy = pltpu.make_async_remote_copy(
            src_ref=source,
            dst_ref=target,
            send_sem=send_sem,
            recv_sem=recv_sem,
            device_id=to,
            device_id_type=MESH,
        )
        copy.start()
        sends.append(copy)
        return copy

    def start_halo(turn):
        copies = []
        faces_at = (plane, plane + pad_x)
        for k, dx in enumerate((-1, 1)):
            first = 0 if dx < 0 else (node_x - 1) * pad_y
            copies.append(
                send(
                    part.at[turn, :, pl.ds(first, pad_y), :],
                    face_x.at[turn, k],
                    at(dx, 0),
                    halo_send.at[turn, k],
                    halo_recv.at[turn, k],
                )
            )
        for k, dy in enumerate((-1, 1)):
            copies.append(
                send(
                    part.at[turn, :, pl.ds(faces_at[k], pad_x), :],
                    face_y.at[turn, k],
                    at(0, dy),
                    halo_send.at[turn, 2 + k],
                    halo_recv.at[turn, 2 + k],
                )
            )
        for k, (dx, dy) in enumerate(corners):
            copies.append(
                send(
                    part.at[turn, :, pl.ds(faces_at[0 if dy < 0 else 1], pad_x), :],
                    corner.at[turn, k],
                    at(dx, dy),
                    halo_send.at[turn, 4 + k],
                    halo_recv.at[turn, 4 + k],
                )
            )
        return copies

    row_at = lax.broadcasted_iota(jnp.int32, (3, pad_y, 2 * zone_z), 1)

    def finish_halo(turn, copies):
        for copy in copies:
            copy.wait_recv()
        last = node_x - 1
        for x in range(node_x):
            block = part[turn, :, x * pad_y : (x + 1) * pad_y, :]
            low = face_y[turn, 1, :, x : x + 1, :]
            high = face_y[turn, 0, :, x : x + 1, :]
            if x == 0:
                block = block + face_x[turn, 1]
                low = low + corner[turn, 3, :, last : last + 1, :]
                high = high + corner[turn, 2, :, last : last + 1, :]
            if x == last:
                block = block + face_x[turn, 0]
                low = low + corner[turn, 1, :, 0:1, :]
                high = high + corner[turn, 0, :, 0:1, :]
            block = block + jnp.where(row_at == 0, low, jnp.where(row_at == node_y - 1, high, 0.0))
            total[turn, :, x * pad_y : (x + 1) * pad_y, :] = block

    def owned(turn):
        return [
            total[turn, c, x * pad_y : x * pad_y + 2 * zone_y, :]
            for c in range(3)
            for x in range(2 * zone_x)
        ]

    def moment(left, right):
        terms = [a * b for a, b in zip(owned(left), owned(right))]
        while len(terms) > 1:
            terms = [sum(terms[k : k + 2]) for k in range(0, len(terms), 2)]
        return jnp.sum(terms[0], axis=0, keepdims=True)

    side_xy = product(
        plane_slopes_t[...],
        split_rows(jnp.concatenate([stress[0], stress[1]], axis=0)),
    )
    side_z = product(plane_value_t[...], split_rows(stress[2]))
    rows_part = plane + 2 * pad_x
    both = jnp.concatenate([rows_of(side_xy, lanes), rows_of(side_z, lanes)], axis=1)
    part[0] = product(split_lanes(both), depth_both_t[...]).reshape(3, rows_part, 2 * zone_z)
    pl.semaphore_wait(barrier, len(others))
    copies = start_halo(0)

    mass_weight = weight_table[...] * rho[...]
    gradients(1)
    work = jnp.zeros((wide, lanes), jnp.float32)
    for c in range(3):
        for d in range(3):
            work = work + jac[d, :, c * lanes : (c + 1) * lanes] * stress[d, :, c * lanes : (c + 1) * lanes]

    def to_linear(x):
        results = []
        for jx in range(2):
            for jy in range(2):
                acc = jnp.zeros((tile, lanes), jnp.float32)
                for a in range(3):
                    for b in range(3):
                        t = a * 3 + b
                        acc = acc + float(linear_one[a, jx] * linear_one[b, jy]) * x[t * tile : (t + 1) * tile]
                for jz in range(2):
                    scaled = acc * (upper if jz else 1.0 - upper)
                    folded = scaled[:, : 2 * zone_z] + scaled[:, 2 * zone_z :]
                    results.append(folded + pltpu.roll(folded, zone_z, 1))
        return results

    rates = to_linear(work)
    lumped = to_linear(mass_weight)
    for j in range(8):
        rate = -rates[j] / lumped[j]
        for x in range(zone_x):
            energy_rate[j, x] = rate[x * zone_y : (x + 1) * zone_y, :zone_z]

    finish_halo(0, copies)
    moments = [moment(0, 0)]
    weight_three = jnp.concatenate([mass_weight] * 3, axis=1)
    for turn in range(1, ROUNDS):
        source = split_lanes(total[turn - 1].reshape(3 * plane, 2 * zone_z))
        nodes = split_rows(lanes_of(product(source, depth_value[...]), plane))
        at_points = product(plane_value[...], nodes) * weight_three
        back = product(plane_value_t[...], split_rows(at_points))
        part[turn] = product(split_lanes(rows_of(back, lanes)), depth_value_t[...]).reshape(
            3, rows_part, 2 * zone_z
        )
        copies = start_halo(turn)
        if turn > 1:
            moments += [moment(turn - 2, turn - 1), moment(turn - 1, turn - 1)]
        finish_halo(turn, copies)
    moments.append(moment(ROUNDS - 2, ROUNDS - 1))

    fill = jnp.zeros((8 - len(moments), 2 * zone_z), jnp.float32)
    dom_parts[0] = jnp.concatenate(moments + [fill], axis=0)
    copies = [
        send(dom_parts.at[0], dom_parts.at[k], at(k, 0), dom_send.at[k], dom_recv.at[k])
        for k in range(1, n_dom)
    ]
    for copy in copies:
        copy.wait_recv()
    sub_parts[0] = jnp.sum(dom_parts[...], axis=0)
    copies = [
        send(sub_parts.at[0], sub_parts.at[k], at(0, k), sub_send.at[k], sub_recv.at[k])
        for k in range(1, n_sub)
    ]
    for copy in copies:
        copy.wait_recv()
    summed = jnp.sum(jnp.sum(sub_parts[...], axis=0), axis=1, keepdims=True)
    mom = [jnp.broadcast_to(summed[k : k + 1], (1, 2 * zone_z)) for k in range(2 * CG_ITERS)]

    def inner(left, right, shift):
        acc = None
        for i, a in enumerate(left):
            for j, b in enumerate(right):
                term = a * b * mom[i + j + shift]
                acc = term if acc is None else acc + term
        return acc

    def combine(left, right, factor):
        out = []
        for k in range(max(len(left), len(right))):
            if k >= len(right):
                out.append(left[k])
            elif k >= len(left):
                out.append(factor * right[k])
            else:
                out.append(left[k] + factor * right[k])
        return out

    one = jnp.ones((1, 2 * zone_z), jnp.float32)
    nil = jnp.zeros((1, 2 * zone_z), jnp.float32)
    answer, rest, direction = [], [one], [one]
    norm = mom[0]
    for sweep in range(CG_ITERS):
        step = norm / inner(direction, direction, 1)
        answer = combine(answer, direction, step)
        rest = combine(rest, [nil] + direction, -step)
        if sweep + 1 < CG_ITERS:
            norm_next = inner(rest, rest, 0)
            direction = combine(rest, direction, norm_next / norm)
            norm = norm_next
    for c in range(3):
        for x in range(node_x):
            basis = [total[k, c, x * pad_y : x * pad_y + node_y, :] for k in range(ROUNDS)]
            accel[c, x] = sum(answer[k] * basis[k] for k in range(CG_ITERS))
            residual[c, x] = sum(rest[k] * basis[k] for k in range(ROUNDS))
    for copy in sends:
        copy.wait_send()


def per_device(
    velocity, displacement, energy, rho_weight, mass_share, energy_share, material_id, mix_mask
):
    n_dom, n_sub = lax.axis_size("dom"), lax.axis_size("sub")
    zone_x, zone_y, zone_z = energy.shape[1:]
    node_x, node_y = 2 * zone_x + 1, 2 * zone_y + 1
    pad_x, pad_y = round_up(node_x, 8), round_up(node_y, 8)
    lanes = 4 * zone_z
    plane, wide, tile = node_x * pad_y, 9 * zone_x * zone_y, zone_x * zone_y
    rows_part = plane + 2 * pad_x
    dims = (n_dom, n_sub, zone_x, zone_y, zone_z, pad_x, pad_y, lanes)

    z_value = depth_matrix(value_one, zone_z, lanes)
    z_slope = depth_matrix(slope_one, zone_z, lanes)
    xy = [
        plane_matrix(first, second, zone_x, zone_y, pad_y)
        for first, second in ((value_one, value_one), (slope_one, value_one), (value_one, slope_one))
    ]
    xy_t = [with_faces(table, zone_x, zone_y, pad_y, pad_x) for table in xy]
    weights = np.zeros((9, tile, 4, zone_z), np.float32)
    for a in range(3):
        for b in range(3):
            for q in range(3):
                weights[a * 3 + b, :, q] = quad_one[a] * quad_one[b] * quad_one[q]
    tables = (
        split_table(z_value, 0),
        split_table(z_slope, 0),
        split_table(z_value.T, 0),
        split_table(np.concatenate([z_value.T, z_slope.T], 0), 0),
        split_table(xy[0], 1),
        split_table(np.concatenate([xy[1], xy[2]], 0), 1),
        split_table(xy_t[0], 1),
        split_table(np.concatenate([xy_t[1], xy_t[2]], 1), 1),
        weights.reshape(wide, lanes),
    )
    f32 = jnp.float32
    vmem = pl.BlockSpec(memory_space=pltpu.VMEM)
    return pl.pallas_call(
        functools.partial(kernel, dims),
        out_shape=(
            jax.ShapeDtypeStruct(velocity.shape, f32),
            jax.ShapeDtypeStruct(velocity.shape, f32),
            jax.ShapeDtypeStruct(energy.shape, f32),
        ),
        in_specs=[vmem] * (8 + len(tables)),
        out_specs=(vmem,) * 3,
        scratch_shapes=[
            pltpu.VMEM((2, 3, plane, 2 * zone_z), f32),
            pltpu.VMEM((wide, lanes), f32),
            pltpu.VMEM((3 * MATS + 8, tile, 2 * zone_z), f32),
            pltpu.VMEM((3, wide, 3 * lanes), f32),
            pltpu.VMEM((3, wide, 3 * lanes), f32),
            pltpu.VMEM((ROUNDS, 3, rows_part, 2 * zone_z), f32),
            pltpu.VMEM((ROUNDS, 3, plane, 2 * zone_z), f32),
            pltpu.VMEM((ROUNDS, 2, 3, pad_y, 2 * zone_z), f32),
            pltpu.VMEM((ROUNDS, 2, 3, pad_x, 2 * zone_z), f32),
            pltpu.VMEM((ROUNDS, 4, 3, pad_x, 2 * zone_z), f32),
            pltpu.VMEM((n_dom, 8, 2 * zone_z), f32),
            pltpu.VMEM((n_sub, 8, 2 * zone_z), f32),
            pltpu.SemaphoreType.DMA((ROUNDS, 8)),
            pltpu.SemaphoreType.DMA((ROUNDS, 8)),
            pltpu.SemaphoreType.DMA((n_dom,)),
            pltpu.SemaphoreType.DMA((n_dom,)),
            pltpu.SemaphoreType.DMA((n_sub,)),
            pltpu.SemaphoreType.DMA((n_sub,)),
        ],
        compiler_params=pltpu.CompilerParams(
            collective_id=0, has_side_effects=True, vmem_limit_bytes=32 * 2**20
        ),
    )(
        velocity,
        displacement,
        energy,
        rho_weight,
        mass_share,
        energy_share,
        material_id,
        mix_mask,
        *[jnp.asarray(table) for table in tables],
    )


def solution(mesh):
    blocks = P(None, "dom", "sub", None)
    return jax.shard_map(
        per_device,
        mesh=mesh,
        in_specs=(blocks,) * 6 + (P("dom", "sub", None), blocks),
        out_specs=(blocks,) * 3,
        check_vma=False,
    )
```

```python
import functools
import math

import jax
import jax.numpy as jnp
import numpy as np
from jax import lax
from jax.experimental import pallas as pl
from jax.experimental.pallas import tpu as pltpu
from jax.sharding import PartitionSpec as P
import ml_dtypes

MESH = pl.DeviceIdType.MESH
MATS = 4
EQ_ITERS = 4
CG_ITERS = 3
ROUNDS = CG_ITERS + 1
N_INPUTS = 17

gammas = (1.4, 1.67, 2.0, 3.0)
cold_terms = (0.3, 1.2, 0.6, 2.4)

spread_root = math.sqrt(0.15)
points = np.array([0.5 - spread_root, 0.5, 0.5 + spread_root])
quad_one = np.array([5.0, 8.0, 5.0]) / 18.0
value_one = np.stack(
    [
        2.0 * (points - 0.5) * (points - 1.0),
        -4.0 * points * (points - 1.0),
        2.0 * points * (points - 0.5),
    ],
    1,
)
slope_one = np.stack([4.0 * points - 3.0, 4.0 - 8.0 * points, 4.0 * points - 1.0], 1)
linear_one = np.stack([1.0 - points, points], 1)


def round_up(value, step):
    return -(-value // step) * step


def split_table(table, axis):
    table = table.astype(np.float32)
    high = table.astype(ml_dtypes.bfloat16)
    low = (table - high.astype(np.float32)).astype(ml_dtypes.bfloat16)
    return np.concatenate([high, high, low], axis)


def depth_matrix(one, zone_z, lanes):
    table = np.zeros((2 * zone_z, lanes))
    for q in range(3):
        for z in range(zone_z):
            for k in range(3):
                table[(2 * z + k) % (2 * zone_z), q * zone_z + z] += one[q, k]
    return table


def plane_matrix(one_x, one_y, zone_x, zone_y, pad_y):
    table = np.zeros((9 * zone_x * zone_y, (2 * zone_x + 1) * pad_y))
    for a in range(3):
        for b in range(3):
            for x in range(zone_x):
                for y in range(zone_y):
                    row = ((a * 3 + b) * zone_x + x) * zone_y + y
                    for i in range(3):
                        for j in range(3):
                            table[row, (2 * x + i) * pad_y + 2 * y + j] = one_x[a, i] * one_y[b, j]
    return table


def split_lanes(x):
    high = x.astype(jnp.bfloat16)
    low = (x - high.astype(jnp.float32)).astype(jnp.bfloat16)
    return jnp.concatenate([high, low, high], axis=1)


def split_rows(x):
    high = x.astype(jnp.bfloat16).astype(jnp.float32)
    return jnp.concatenate([high, x - high, high], axis=0).astype(jnp.bfloat16)


def product(left, right):
    return jnp.dot(left, right, preferred_element_type=jnp.float32)


def lanes_of(x, rows):
    return jnp.concatenate([x[c * rows : (c + 1) * rows] for c in range(3)], axis=1)


def rows_of(x, lanes):
    return jnp.concatenate([x[:, c * lanes : (c + 1) * lanes] for c in range(3)], axis=0)


def kernel(
    dims,
    *refs,
):
    outer, refs = refs[:N_INPUTS], refs[N_INPUTS:]
    outputs, refs = refs[:3], refs[3:]
    inner, refs = refs[:N_INPUTS], refs[N_INPUTS:]
    body(dims, outer, *inner, *outputs, *refs)


def body(
    dims,
    outer,
    displacement,
    depth_value,
    depth_slope,
    plane_slopes,
    plane_value,
    material_id,
    mix_mask,
    mass_share,
    energy_share,
    energy,
    rho_weight,
    weight_table,
    plane_slopes_t,
    plane_value_t,
    depth_both_t,
    velocity,
    depth_value_t,
    accel,
    residual,
    energy_rate,
    load_sem,
    field,
    rho,
    zone_in,
    jac,
    stress,
    part,
    total,
    side_y,
    side_corner,
    face_x,
    face_y,
    corner,
    dom_parts,
    sub_parts,
    halo_send,
    halo_recv,
    dom_send,
    dom_recv,
    sub_send,
    sub_recv,
):
    n_dom, n_sub, zone_x, zone_y, zone_z, pad_x, pad_y, lanes = dims
    node_x, node_y = 2 * zone_x + 1, 2 * zone_y + 1
    plane = node_x * pad_y
    tile = zone_x * zone_y
    wide = 9 * tile
    me_dom, me_sub = lax.axis_index("dom"), lax.axis_index("sub")

    def at(shift_dom, shift_sub):
        return (lax.rem(me_dom + shift_dom + n_dom, n_dom), lax.rem(me_sub + shift_sub + n_sub, n_sub))

    corners = [(-1, -1), (-1, 1), (1, -1), (1, 1)]
    others = [at(k, 0) for k in range(1, n_dom)] + [at(0, k) for k in range(1, n_sub)]
    others += [at(dx, dy) for dx, dy in corners]
    barrier = pltpu.get_barrier_semaphore()
    for other in others:
        pl.semaphore_signal(barrier, inc=1, device_id=other, device_id_type=MESH)

    def gradients(which):
        source = split_lanes(field[which].reshape(3 * plane, 2 * zone_z))
        by_value = split_rows(lanes_of(product(source, depth_value[...]), plane))
        by_slope = split_rows(lanes_of(product(source, depth_slope[...]), plane))
        along_xy = product(plane_slopes[...], by_value)
        along_z = product(plane_value[...], by_slope)
        jac[0] = along_xy[:wide]
        jac[1] = along_xy[wide:]
        jac[2] = along_z

    inner = (
        displacement, depth_value, depth_slope, plane_slopes, plane_value, material_id, mix_mask,
        mass_share, energy_share, energy, rho_weight, weight_table, plane_slopes_t, plane_value_t,
        depth_both_t, velocity, depth_value_t,
    )
    loads = [pltpu.make_async_copy(a, b, load_sem.at[k]) for k, (a, b) in enumerate(zip(outer, inner))]
    for load in loads:
        load.start()
    field[...] = jnp.zeros_like(field)
    for load in loads[:5]:
        load.wait()

    def unpack(which, source):
        for x in range(node_x):
            for c in range(3):
                field[which, c, x * pad_y : x * pad_y + node_y, :] = source[x, :, c, :]

    unpack(0, displacement)
    gradients(0)
    for load in loads[5:]:
        load.wait()
    for t in range(9):
        for q in range(4):
            for x in range(zone_x):
                rho[t * tile + x * zone_y : t * tile + (x + 1) * zone_y, q * zone_z : (q + 1) * zone_z] = (
                    rho_weight[3 * t + q % 3, x]
                )
    for half in range(2):
        cols = slice(half * zone_z, (half + 1) * zone_z)
        for x in range(zone_x):
            rows = slice(x * zone_y, (x + 1) * zone_y)
            for m in range(MATS):
                present = jnp.where((mix_mask[m, x] == 1) | (material_id[x] == m), 1.0, 0.0)
                zone_in[m, rows, cols] = present
                zone_in[MATS + m, rows, cols] = mass_share[m, x]
                zone_in[2 * MATS + m, rows, cols] = energy_share[m, x]
            for j in range(8):
                zone_in[3 * MATS + j, rows, cols] = energy[j, x]

    present = [zone_in[m] for m in range(MATS)]
    weighted = [present[m] * zone_in[MATS + m] for m in range(MATS)]
    weighted_sum = 1.0 / (weighted[0] + weighted[1] + weighted[2] + weighted[3])
    present_sum = 1.0 / (present[0] + present[1] + present[2] + present[3])

    def spread(x):
        return jnp.concatenate([jnp.concatenate([x, x], axis=1)] * 3, axis=0)

    start = [spread(present[m] * present_sum) for m in range(MATS)]
    load = [
        spread((gammas[m] - 1.0) * (weighted[m] * weighted_sum) * zone_in[2 * MATS + m])
        for m in range(MATS)
    ]
    lane_at = lax.broadcasted_iota(jnp.int32, (tile, lanes), 1) // zone_z
    upper = jnp.where(lane_at == 1, points[1], jnp.where(lane_at == 2, points[2], points[0])).astype(
        jnp.float32
    )
    along = []
    for j in range(4):
        low, high = zone_in[3 * MATS + 2 * j], zone_in[3 * MATS + 2 * j + 1]
        low, high = jnp.concatenate([low, low], axis=1), jnp.concatenate([high, high], axis=1)
        along.append(low + upper * (high - low))

    for a in range(3):
        rows = slice(a * 3 * tile, (a + 1) * 3 * tile)
        x_low = [linear_one[a, 0] * along[jy] + linear_one[a, 1] * along[2 + jy] for jy in range(2)]
        energy_points = jnp.concatenate(
            [linear_one[b, 0] * x_low[0] + linear_one[b, 1] * x_low[1] for b in range(3)], axis=0
        )

        def entry(c, d):
            value = jac[d, rows, c * lanes : (c + 1) * lanes]
            return value + 1.0 if c == d else value

        matrix = [[entry(c, d) for d in range(3)] for c in range(3)]
        adjugate = [[None] * 3 for _ in range(3)]
        for d in range(3):
            for c in range(3):
                adjugate[d][c] = (
                    matrix[(c + 1) % 3][(d + 1) % 3] * matrix[(c + 2) % 3][(d + 2) % 3]
                    - matrix[(c + 1) % 3][(d + 2) % 3] * matrix[(c + 2) % 3][(d + 1) % 3]
                )
        determinant = (
            matrix[0][0] * adjugate[0][0]
            + matrix[0][1] * adjugate[1][0]
            + matrix[0][2] * adjugate[2][0]
        )
        base = rho[rows, :] / determinant * energy_points
        pressure_load = [load[m] * base for m in range(MATS)]
        fraction = list(start)
        for sweep in range(EQ_ITERS):
            grown = []
            for m in range(MATS):
                square = fraction[m] * (pressure_load[m] + cold_terms[m] * fraction[m])
                grown.append(square * lax.rsqrt(jnp.maximum(square, 1e-30)))
            scale = 1.0 / ((grown[0] + grown[1]) + (grown[2] + grown[3]))
            fraction = [grown[m] * scale for m in range(MATS)]
        pressure = (
            (pressure_load[0] + cold_terms[0] * fraction[0])
            + (pressure_load[1] + cold_terms[1] * fraction[1])
            + (pressure_load[2] + cold_terms[2] * fraction[2])
            + (pressure_load[3] + cold_terms[3] * fraction[3])
        )
        weighted_pressure = weight_table[rows, :] * pressure
        for d in range(3):
            for c in range(3):
                stress[d, rows, c * lanes : (c + 1) * lanes] = weighted_pressure * adjugate[d][c]

    sends = []

    def send(source, target, to, send_sem, recv_sem):
        copy = pltpu.make_async_remote_copy(
            src_ref=source,
            dst_ref=target,
            send_sem=send_sem,
            recv_sem=recv_sem,
            device_id=to,
            device_id_type=MESH,
        )
        copy.start()
        sends.append(copy)
        return copy

    last = node_x - 1

    def start_halo(turn):
        for k in range(2):
            row = k * (node_y - 1)
            for x in range(node_x):
                for c in range(3):
                    line = part[turn, c, x * pad_y + row : x * pad_y + row + 1, :]
                    side_y[turn, k, x, c] = line
                    if x == 0:
                        side_corner[turn, k, c] = line
                    if x == last:
                        side_corner[turn, 2 + k, c] = line
        copies = []
        for k, (dx, dy) in enumerate(corners):
            copies.append(
                send(
                    side_corner.at[turn, k],
                    corner.at[turn, k],
                    at(dx, dy),
                    halo_send.at[turn, 4 + k],
                    halo_recv.at[turn, 4 + k],
                )
            )
        for k, dy in enumerate((-1, 1)):
            copies.append(
                send(
                    side_y.at[turn, k],
                    face_y.at[turn, k],
                    at(0, dy),
                    halo_send.at[turn, 2 + k],
                    halo_recv.at[turn, 2 + k],
                )
            )
        for k, dx in enumerate((-1, 1)):
            first = 0 if dx < 0 else last * pad_y
            copies.append(
                send(
                    part.at[turn, :, pl.ds(first, pad_y), :],
                    face_x.at[turn, k],
                    at(dx, 0),
                    halo_send.at[turn, k],
                    halo_recv.at[turn, k],
                )
            )
        return copies

    row_at = lax.broadcasted_iota(jnp.int32, (pad_y, 2 * zone_z), 0)

    def finish_halo(turn, copies):
        for copy in copies:
            copy.wait_recv()
        for x in range(node_x):
            for c in range(3):
                block = part[turn, c, x * pad_y : (x + 1) * pad_y, :]
                low = face_y[turn, 1, x, c]
                high = face_y[turn, 0, x, c]
                if x == 0:
                    block = block + face_x[turn, 1, c]
                    low = low + corner[turn, 3, c]
                    high = high + corner[turn, 2, c]
                if x == last:
                    block = block + face_x[turn, 0, c]
                    low = low + corner[turn, 1, c]
                    high = high + corner[turn, 0, c]
                block = block + jnp.where(row_at == 0, low, jnp.where(row_at == node_y - 1, high, 0.0))
                total[turn, c, x * pad_y : (x + 1) * pad_y, :] = block

    def owned(turn):
        return [
            total[turn, c, x * pad_y : x * pad_y + 2 * zone_y, :]
            for c in range(3)
            for x in range(2 * zone_x)
        ]

    def tree(terms):
        while len(terms) > 1:
            terms = [sum(terms[k : k + 2]) for k in range(0, len(terms), 2)]
        return jnp.sum(terms[0], axis=0, keepdims=True)

    def square(turn):
        return tree([a * a for a in owned(turn)])

    def energy_of(at_points, scaled):
        both = at_points * scaled
        return tree(
            [
                both[t * tile : (t + 1) * tile, k * 2 * zone_z : (k + 1) * 2 * zone_z]
                for t in range(9)
                for k in range(3 * lanes // (2 * zone_z))
            ]
        )

    side_xy = product(
        plane_slopes_t[...],
        split_rows(jnp.concatenate([stress[0], stress[1]], axis=0)),
    )
    side_z = product(plane_value_t[...], split_rows(stress[2]))
    both = jnp.concatenate([rows_of(side_xy, lanes), rows_of(side_z, lanes)], axis=1)
    part[0] = product(split_lanes(both), depth_both_t[...]).reshape(3, plane, 2 * zone_z)
    pl.semaphore_wait(barrier, len(others))
    copies = start_halo(0)

    mass_weight = weight_table[...] * rho[...]
    unpack(1, velocity)
    gradients(1)
    work = jnp.zeros((wide, lanes), jnp.float32)
    for c in range(3):
        for d in range(3):
            work = work + jac[d, :, c * lanes : (c + 1) * lanes] * stress[d, :, c * lanes : (c + 1) * lanes]

    def to_linear(x):
        results = []
        for jx in range(2):
            for jy in range(2):
                acc = jnp.zeros((tile, lanes), jnp.float32)
                for a in range(3):
                    for b in range(3):
                        t = a * 3 + b
                        acc = acc + float(linear_one[a, jx] * linear_one[b, jy]) * x[t * tile : (t + 1) * tile]
                for jz in range(2):
                    scaled = acc * (upper if jz else 1.0 - upper)
                    folded = scaled[:, : 2 * zone_z] + scaled[:, 2 * zone_z :]
                    results.append(folded + pltpu.roll(folded, zone_z, 1))
        return results

    rates = to_linear(work)
    lumped = to_linear(mass_weight)
    for j in range(8):
        rate = -rates[j] / lumped[j]
        for x in range(zone_x):
            energy_rate[j, x] = rate[x * zone_y : (x + 1) * zone_y, :zone_z]

    finish_halo(0, copies)
    moments = []
    weight_three = jnp.concatenate([mass_weight] * 3, axis=1)
    for turn in range(1, ROUNDS):
        source = split_lanes(total[turn - 1].reshape(3 * plane, 2 * zone_z))
        nodes = split_rows(lanes_of(product(source, depth_value[...]), plane))
        at_points = product(plane_value[...], nodes)
        scaled = at_points * weight_three
        if turn == ROUNDS - 1:
            moments += [square(turn - 1), energy_of(at_points, scaled)]
            fill = jnp.zeros((8 - len(moments), 2 * zone_z), jnp.float32)
            dom_parts[0] = jnp.concatenate(moments + [fill], axis=0)
            dom_copies = [
                send(dom_parts.at[0], dom_parts.at[k], at(k, 0), dom_send.at[k], dom_recv.at[k])
                for k in range(1, n_dom)
            ]
        back = product(plane_value_t[...], split_rows(scaled))
        part[turn] = product(split_lanes(rows_of(back, lanes)), depth_value_t[...]).reshape(
            3, plane, 2 * zone_z
        )
        copies = start_halo(turn)
        if turn < ROUNDS - 1:
            moments += [square(turn - 1), energy_of(at_points, scaled)]
            finish_halo(turn, copies)
    for copy in dom_copies:
        copy.wait_recv()
    sub_parts[0] = jnp.sum(dom_parts[...], axis=0)
    sub_copies = [
        send(sub_parts.at[0], sub_parts.at[k], at(0, k), sub_send.at[k], sub_recv.at[k])
        for k in range(1, n_sub)
    ]
    finish_halo(ROUNDS - 1, copies)
    for copy in sub_copies:
        copy.wait_recv()
    summed = jnp.sum(jnp.sum(sub_parts[...], axis=0), axis=1, keepdims=True)
    mom = [jnp.broadcast_to(summed[k : k + 1], (1, 2 * zone_z)) for k in range(2 * CG_ITERS)]

    def inner(left, right, shift):
        acc = None
        for i, a in enumerate(left):
            for j, b in enumerate(right):
                term = a * b * mom[i + j + shift]
                acc = term if acc is None else acc + term
        return acc

    def combine(left, right, factor):
        out = []
        for k in range(max(len(left), len(right))):
            if k >= len(right):
                out.append(left[k])
            elif k >= len(left):
                out.append(factor * right[k])
            else:
                out.append(left[k] + factor * right[k])
        return out

    one = jnp.ones((1, 2 * zone_z), jnp.float32)
    nil = jnp.zeros((1, 2 * zone_z), jnp.float32)
    answer, rest, direction = [], [one], [one]
    norm = mom[0]
    for sweep in range(CG_ITERS):
        step = norm / inner(direction, direction, 1)
        answer = combine(answer, direction, step)
        rest = combine(rest, [nil] + direction, -step)
        if sweep + 1 < CG_ITERS:
            norm_next = inner(rest, rest, 0)
            direction = combine(rest, direction, norm_next / norm)
            norm = norm_next
    for c in range(3):
        for x in range(node_x):
            basis = [total[k, c, x * pad_y : x * pad_y + node_y, :] for k in range(ROUNDS)]
            accel[x, :, c, :] = sum(answer[k] * basis[k] for k in range(CG_ITERS))
            residual[x, :, c, :] = sum(rest[k] * basis[k] for k in range(ROUNDS))
    for copy in sends:
        copy.wait_send()


def per_device(
    velocity, displacement, energy, rho_weight, mass_share, energy_share, material_id, mix_mask
):
    n_dom, n_sub = lax.axis_size("dom"), lax.axis_size("sub")
    zone_x, zone_y, zone_z = energy.shape[1:]
    node_x, node_y = 2 * zone_x + 1, 2 * zone_y + 1
    pad_x, pad_y = round_up(node_x, 8), round_up(node_y, 8)
    lanes = 4 * zone_z
    plane, wide, tile = node_x * pad_y, 9 * zone_x * zone_y, zone_x * zone_y
    dims = (n_dom, n_sub, zone_x, zone_y, zone_z, pad_x, pad_y, lanes)

    z_value = depth_matrix(value_one, zone_z, lanes)
    z_slope = depth_matrix(slope_one, zone_z, lanes)
    xy = [
        plane_matrix(first, second, zone_x, zone_y, pad_y)
        for first, second in ((value_one, value_one), (slope_one, value_one), (value_one, slope_one))
    ]
    xy_t = [table.T for table in xy]
    weights = np.zeros((9, tile, 4, zone_z), np.float32)
    for a in range(3):
        for b in range(3):
            for q in range(3):
                weights[a * 3 + b, :, q] = quad_one[a] * quad_one[b] * quad_one[q]
    order = (1, 2, 0, 3)
    inputs = (
        jnp.transpose(displacement, order),
        split_table(z_value, 0),
        split_table(z_slope, 0),
        split_table(np.concatenate([xy[1], xy[2]], 0), 1),
        split_table(xy[0], 1),
        material_id,
        mix_mask,
        mass_share,
        energy_share,
        energy,
        rho_weight,
        weights.reshape(wide, lanes),
        split_table(np.concatenate([xy_t[1], xy_t[2]], 1), 1),
        split_table(xy_t[0], 1),
        split_table(np.concatenate([z_value.T, z_slope.T], 0), 0),
        jnp.transpose(velocity, order),
        split_table(z_value.T, 0),
    )
    inputs = [jnp.asarray(array) for array in inputs]
    f32 = jnp.float32
    vmem = pl.BlockSpec(memory_space=pltpu.VMEM)
    nodes_out = jax.ShapeDtypeStruct((node_x, node_y, 3, 2 * zone_z), f32)
    accel, residual, energy_rate = pl.pallas_call(
        functools.partial(kernel, dims),
        out_shape=(nodes_out, nodes_out, jax.ShapeDtypeStruct(energy.shape, f32)),
        in_specs=[pl.BlockSpec(memory_space=pltpu.HBM)] * N_INPUTS,
        out_specs=(vmem,) * 3,
        scratch_shapes=[pltpu.VMEM(array.shape, array.dtype) for array in inputs]
        + [
            pltpu.SemaphoreType.DMA((N_INPUTS,)),
            pltpu.VMEM((2, 3, plane, 2 * zone_z), f32),
            pltpu.VMEM((wide, lanes), f32),
            pltpu.VMEM((3 * MATS + 8, tile, 2 * zone_z), f32),
            pltpu.VMEM((3, wide, 3 * lanes), f32),
            pltpu.VMEM((3, wide, 3 * lanes), f32),
            pltpu.VMEM((ROUNDS, 3, plane, 2 * zone_z), f32),
            pltpu.VMEM((ROUNDS, 3, plane, 2 * zone_z), f32),
            pltpu.VMEM((ROUNDS, 2, node_x, 3, 1, 2 * zone_z), f32),
            pltpu.VMEM((ROUNDS, 4, 3, 1, 2 * zone_z), f32),
            pltpu.VMEM((ROUNDS, 2, 3, pad_y, 2 * zone_z), f32),
            pltpu.VMEM((ROUNDS, 2, node_x, 3, 1, 2 * zone_z), f32),
            pltpu.VMEM((ROUNDS, 4, 3, 1, 2 * zone_z), f32),
            pltpu.VMEM((n_dom, 8, 2 * zone_z), f32),
            pltpu.VMEM((n_sub, 8, 2 * zone_z), f32),
            pltpu.SemaphoreType.DMA((ROUNDS, 8)),
            pltpu.SemaphoreType.DMA((ROUNDS, 8)),
            pltpu.SemaphoreType.DMA((n_dom,)),
            pltpu.SemaphoreType.DMA((n_dom,)),
            pltpu.SemaphoreType.DMA((n_sub,)),
            pltpu.SemaphoreType.DMA((n_sub,)),
        ],
        compiler_params=pltpu.CompilerParams(
            collective_id=0, has_side_effects=True, vmem_limit_bytes=60 * 2**20
        ),
    )(*inputs)
    back = (2, 0, 1, 3)
    return jnp.transpose(accel, back), jnp.transpose(residual, back), energy_rate


def solution(mesh):
    blocks = P(None, "dom", "sub", None)
    return jax.shard_map(
        per_device,
        mesh=mesh,
        in_specs=(blocks,) * 6 + (P("dom", "sub", None), blocks),
        out_specs=(blocks,) * 3,
        check_vma=False,
    )
```

```python
import functools
import math

import jax
import jax.numpy as jnp
import numpy as np
from jax import lax
from jax.experimental import pallas as pl
from jax.experimental.pallas import tpu as pltpu
from jax.sharding import PartitionSpec as P
import ml_dtypes

MESH = pl.DeviceIdType.MESH
MATS = 4
EQ_ITERS = 4
CG_ITERS = 3
ROUNDS = CG_ITERS + 1
N_INPUTS = 17

gammas = (1.4, 1.67, 2.0, 3.0)
cold_terms = (0.3, 1.2, 0.6, 2.4)

spread_root = math.sqrt(0.15)
points = np.array([0.5 - spread_root, 0.5, 0.5 + spread_root])
quad_one = np.array([5.0, 8.0, 5.0]) / 18.0
value_one = np.stack(
    [
        2.0 * (points - 0.5) * (points - 1.0),
        -4.0 * points * (points - 1.0),
        2.0 * points * (points - 0.5),
    ],
    1,
)
slope_one = np.stack([4.0 * points - 3.0, 4.0 - 8.0 * points, 4.0 * points - 1.0], 1)
linear_one = np.stack([1.0 - points, points], 1)


def round_up(value, step):
    return -(-value // step) * step


def split_table(table, axis):
    table = table.astype(np.float32)
    high = table.astype(ml_dtypes.bfloat16)
    low = (table - high.astype(np.float32)).astype(ml_dtypes.bfloat16)
    return np.concatenate([high, high, low], axis)


def depth_matrix(one, zone_z, lanes):
    table = np.zeros((2 * zone_z, lanes))
    for q in range(3):
        for z in range(zone_z):
            for k in range(3):
                table[(2 * z + k) % (2 * zone_z), q * zone_z + z] += one[q, k]
    return table


def plane_matrix(one_x, one_y, zone_x, zone_y, pad_y):
    table = np.zeros((9 * zone_x * zone_y, (2 * zone_x + 1) * pad_y))
    for a in range(3):
        for b in range(3):
            for x in range(zone_x):
                for y in range(zone_y):
                    row = ((a * 3 + b) * zone_x + x) * zone_y + y
                    for i in range(3):
                        for j in range(3):
                            table[row, (2 * x + i) * pad_y + 2 * y + j] = one_x[a, i] * one_y[b, j]
    return table


def split_lanes(x):
    high = x.astype(jnp.bfloat16)
    low = (x - high.astype(jnp.float32)).astype(jnp.bfloat16)
    return jnp.concatenate([high, low, high], axis=1)


def split_rows(x):
    high = x.astype(jnp.bfloat16).astype(jnp.float32)
    return jnp.concatenate([high, x - high, high], axis=0).astype(jnp.bfloat16)


def product(left, right):
    return jnp.dot(left, right, preferred_element_type=jnp.float32)


def lanes_of(x, rows):
    return jnp.concatenate([x[c * rows : (c + 1) * rows] for c in range(3)], axis=1)


def rows_of(x, lanes):
    return jnp.concatenate([x[:, c * lanes : (c + 1) * lanes] for c in range(3)], axis=0)


def kernel(
    dims,
    *refs,
):
    outer, refs = refs[:N_INPUTS], refs[N_INPUTS:]
    outputs, refs = refs[:3], refs[3:]
    inner, refs = refs[:N_INPUTS], refs[N_INPUTS:]
    body(dims, outer, *inner, *outputs, *refs)


def body(
    dims,
    outer,
    displacement,
    depth_value,
    depth_slope,
    plane_slopes,
    plane_value,
    material_id,
    mix_mask,
    mass_share,
    energy_share,
    energy,
    rho_weight,
    weight_table,
    plane_slopes_t,
    plane_value_t,
    depth_both_t,
    velocity,
    depth_value_t,
    total,
    factors,
    energy_rate,
    load_sem,
    field,
    rho,
    zone_in,
    jac,
    stress,
    part,
    side_y,
    side_corner,
    face_x,
    face_y,
    corner,
    dom_parts,
    sub_parts,
    halo_send,
    halo_recv,
    dom_send,
    dom_recv,
    sub_send,
    sub_recv,
):
    n_dom, n_sub, zone_x, zone_y, zone_z, pad_x, pad_y, lanes = dims
    node_x, node_y = 2 * zone_x + 1, 2 * zone_y + 1
    plane = node_x * pad_y
    tile = zone_x * zone_y
    wide = 9 * tile
    me_dom, me_sub = lax.axis_index("dom"), lax.axis_index("sub")

    def at(shift_dom, shift_sub):
        return (lax.rem(me_dom + shift_dom + n_dom, n_dom), lax.rem(me_sub + shift_sub + n_sub, n_sub))

    corners = [(-1, -1), (-1, 1), (1, -1), (1, 1)]
    others = [at(k, 0) for k in range(1, n_dom)] + [at(0, k) for k in range(1, n_sub)]
    others += [at(dx, dy) for dx, dy in corners]
    barrier = pltpu.get_barrier_semaphore()
    for other in others:
        pl.semaphore_signal(barrier, inc=1, device_id=other, device_id_type=MESH)

    def gradients(which):
        source = split_lanes(field[which].reshape(3 * plane, 2 * zone_z))
        by_value = split_rows(lanes_of(product(source, depth_value[...]), plane))
        by_slope = split_rows(lanes_of(product(source, depth_slope[...]), plane))
        along_xy = product(plane_slopes[...], by_value)
        along_z = product(plane_value[...], by_slope)
        jac[0] = along_xy[:wide]
        jac[1] = along_xy[wide:]
        jac[2] = along_z

    inner = (
        displacement, depth_value, depth_slope, plane_slopes, plane_value, material_id, mix_mask,
        mass_share, energy_share, energy, rho_weight, weight_table, plane_slopes_t, plane_value_t,
        depth_both_t, velocity, depth_value_t,
    )
    loads = [pltpu.make_async_copy(a, b, load_sem.at[k]) for k, (a, b) in enumerate(zip(outer, inner))]
    for load in loads:
        load.start()
    field[...] = jnp.zeros_like(field)
    for load in loads[:5]:
        load.wait()

    def unpack(which, source):
        for x in range(node_x):
            for c in range(3):
                field[which, c, x * pad_y : x * pad_y + node_y, :] = source[x, :, c, :]

    unpack(0, displacement)
    gradients(0)
    for load in loads[5:]:
        load.wait()
    for t in range(9):
        for q in range(4):
            for x in range(zone_x):
                rho[t * tile + x * zone_y : t * tile + (x + 1) * zone_y, q * zone_z : (q + 1) * zone_z] = (
                    rho_weight[3 * t + q % 3, x]
                )
    for half in range(2):
        cols = slice(half * zone_z, (half + 1) * zone_z)
        for x in range(zone_x):
            rows = slice(x * zone_y, (x + 1) * zone_y)
            for m in range(MATS):
                present = jnp.where((mix_mask[m, x] == 1) | (material_id[x] == m), 1.0, 0.0)
                zone_in[m, rows, cols] = present
                zone_in[MATS + m, rows, cols] = mass_share[m, x]
                zone_in[2 * MATS + m, rows, cols] = energy_share[m, x]
            for j in range(8):
                zone_in[3 * MATS + j, rows, cols] = energy[j, x]

    present = [zone_in[m] for m in range(MATS)]
    weighted = [present[m] * zone_in[MATS + m] for m in range(MATS)]
    weighted_sum = 1.0 / (weighted[0] + weighted[1] + weighted[2] + weighted[3])
    present_sum = 1.0 / (present[0] + present[1] + present[2] + present[3])

    def spread(x):
        return jnp.concatenate([jnp.concatenate([x, x], axis=1)] * 3, axis=0)

    start = [spread(present[m] * present_sum) for m in range(MATS)]
    load = [
        spread((gammas[m] - 1.0) * (weighted[m] * weighted_sum) * zone_in[2 * MATS + m])
        for m in range(MATS)
    ]
    lane_at = lax.broadcasted_iota(jnp.int32, (tile, lanes), 1) // zone_z
    upper = jnp.where(lane_at == 1, points[1], jnp.where(lane_at == 2, points[2], points[0])).astype(
        jnp.float32
    )
    along = []
    for j in range(4):
        low, high = zone_in[3 * MATS + 2 * j], zone_in[3 * MATS + 2 * j + 1]
        low, high = jnp.concatenate([low, low], axis=1), jnp.concatenate([high, high], axis=1)
        along.append(low + upper * (high - low))

    for a in range(3):
        rows = slice(a * 3 * tile, (a + 1) * 3 * tile)
        x_low = [linear_one[a, 0] * along[jy] + linear_one[a, 1] * along[2 + jy] for jy in range(2)]
        energy_points = jnp.concatenate(
            [linear_one[b, 0] * x_low[0] + linear_one[b, 1] * x_low[1] for b in range(3)], axis=0
        )

        def entry(c, d):
            value = jac[d, rows, c * lanes : (c + 1) * lanes]
            return value + 1.0 if c == d else value

        matrix = [[entry(c, d) for d in range(3)] for c in range(3)]
        adjugate = [[None] * 3 for _ in range(3)]
        for d in range(3):
            for c in range(3):
                adjugate[d][c] = (
                    matrix[(c + 1) % 3][(d + 1) % 3] * matrix[(c + 2) % 3][(d + 2) % 3]
                    - matrix[(c + 1) % 3][(d + 2) % 3] * matrix[(c + 2) % 3][(d + 1) % 3]
                )
        determinant = (
            matrix[0][0] * adjugate[0][0]
            + matrix[0][1] * adjugate[1][0]
            + matrix[0][2] * adjugate[2][0]
        )
        base = rho[rows, :] / determinant * energy_points
        pressure_load = [load[m] * base for m in range(MATS)]
        fraction = list(start)
        for sweep in range(EQ_ITERS):
            grown = []
            for m in range(MATS):
                square = fraction[m] * (pressure_load[m] + cold_terms[m] * fraction[m])
                grown.append(square * lax.rsqrt(jnp.maximum(square, 1e-30)))
            scale = 1.0 / ((grown[0] + grown[1]) + (grown[2] + grown[3]))
            fraction = [grown[m] * scale for m in range(MATS)]
        pressure = (
            (pressure_load[0] + cold_terms[0] * fraction[0])
            + (pressure_load[1] + cold_terms[1] * fraction[1])
            + (pressure_load[2] + cold_terms[2] * fraction[2])
            + (pressure_load[3] + cold_terms[3] * fraction[3])
        )
        weighted_pressure = weight_table[rows, :] * pressure
        for d in range(3):
            for c in range(3):
                stress[d, rows, c * lanes : (c + 1) * lanes] = weighted_pressure * adjugate[d][c]

    sends = []

    def send(source, target, to, send_sem, recv_sem):
        copy = pltpu.make_async_remote_copy(
            src_ref=source,
            dst_ref=target,
            send_sem=send_sem,
            recv_sem=recv_sem,
            device_id=to,
            device_id_type=MESH,
        )
        copy.start()
        sends.append(copy)
        return copy

    last = node_x - 1

    def start_halo(turn):
        for k in range(2):
            row = k * (node_y - 1)
            for x in range(node_x):
                for c in range(3):
                    line = part[turn, c, x * pad_y + row : x * pad_y + row + 1, :]
                    side_y[turn, k, x, c] = line
                    if x == 0:
                        side_corner[turn, k, c] = line
                    if x == last:
                        side_corner[turn, 2 + k, c] = line
        copies = []
        for k, (dx, dy) in enumerate(corners):
            copies.append(
                send(
                    side_corner.at[turn, k],
                    corner.at[turn, k],
                    at(dx, dy),
                    halo_send.at[turn, 4 + k],
                    halo_recv.at[turn, 4 + k],
                )
            )
        for k, dy in enumerate((-1, 1)):
            copies.append(
                send(
                    side_y.at[turn, k],
                    face_y.at[turn, k],
                    at(0, dy),
                    halo_send.at[turn, 2 + k],
                    halo_recv.at[turn, 2 + k],
                )
            )
        for k, dx in enumerate((-1, 1)):
            first = 0 if dx < 0 else last * pad_y
            copies.append(
                send(
                    part.at[turn, :, pl.ds(first, pad_y), :],
                    face_x.at[turn, k],
                    at(dx, 0),
                    halo_send.at[turn, k],
                    halo_recv.at[turn, k],
                )
            )
        return copies

    row_at = lax.broadcasted_iota(jnp.int32, (pad_y, 2 * zone_z), 0)

    def finish_halo(turn, copies):
        for copy in copies:
            copy.wait_recv()
        for x in range(node_x):
            for c in range(3):
                block = part[turn, c, x * pad_y : (x + 1) * pad_y, :]
                low = face_y[turn, 1, x, c]
                high = face_y[turn, 0, x, c]
                if x == 0:
                    block = block + face_x[turn, 1, c]
                    low = low + corner[turn, 3, c]
                    high = high + corner[turn, 2, c]
                if x == last:
                    block = block + face_x[turn, 0, c]
                    low = low + corner[turn, 1, c]
                    high = high + corner[turn, 0, c]
                block = block + jnp.where(row_at == 0, low, jnp.where(row_at == node_y - 1, high, 0.0))
                total[turn, c, x * pad_y : (x + 1) * pad_y, :] = block

    def owned(turn):
        return [
            total[turn, c, x * pad_y : x * pad_y + 2 * zone_y, :]
            for c in range(3)
            for x in range(2 * zone_x)
        ]

    def tree(terms):
        while len(terms) > 1:
            terms = [sum(terms[k : k + 2]) for k in range(0, len(terms), 2)]
        return jnp.sum(terms[0], axis=0, keepdims=True)

    def square(turn):
        return tree([a * a for a in owned(turn)])

    def energy_of(at_points, scaled):
        both = at_points * scaled
        return tree(
            [
                both[t * tile : (t + 1) * tile, k * 2 * zone_z : (k + 1) * 2 * zone_z]
                for t in range(9)
                for k in range(3 * lanes // (2 * zone_z))
            ]
        )

    side_xy = product(
        plane_slopes_t[...],
        split_rows(jnp.concatenate([stress[0], stress[1]], axis=0)),
    )
    side_z = product(plane_value_t[...], split_rows(stress[2]))
    both = jnp.concatenate([rows_of(side_xy, lanes), rows_of(side_z, lanes)], axis=1)
    part[0] = product(split_lanes(both), depth_both_t[...]).reshape(3, plane, 2 * zone_z)
    pl.semaphore_wait(barrier, len(others))
    copies = start_halo(0)

    mass_weight = weight_table[...] * rho[...]
    unpack(1, velocity)
    gradients(1)
    work = jnp.zeros((wide, lanes), jnp.float32)
    for c in range(3):
        for d in range(3):
            work = work + jac[d, :, c * lanes : (c + 1) * lanes] * stress[d, :, c * lanes : (c + 1) * lanes]

    def to_linear(x):
        results = []
        for jx in range(2):
            for jy in range(2):
                acc = jnp.zeros((tile, lanes), jnp.float32)
                for a in range(3):
                    for b in range(3):
                        t = a * 3 + b
                        acc = acc + float(linear_one[a, jx] * linear_one[b, jy]) * x[t * tile : (t + 1) * tile]
                for jz in range(2):
                    scaled = acc * (upper if jz else 1.0 - upper)
                    folded = scaled[:, : 2 * zone_z] + scaled[:, 2 * zone_z :]
                    results.append(folded + pltpu.roll(folded, zone_z, 1))
        return results

    rates = to_linear(work)
    lumped = to_linear(mass_weight)
    for j in range(8):
        rate = -rates[j] / lumped[j]
        for x in range(zone_x):
            energy_rate[j, x] = rate[x * zone_y : (x + 1) * zone_y, :zone_z]

    finish_halo(0, copies)
    moments = []
    weight_three = jnp.concatenate([mass_weight] * 3, axis=1)
    for turn in range(1, ROUNDS):
        source = split_lanes(total[turn - 1].reshape(3 * plane, 2 * zone_z))
        nodes = split_rows(lanes_of(product(source, depth_value[...]), plane))
        at_points = product(plane_value[...], nodes)
        scaled = at_points * weight_three
        if turn == ROUNDS - 1:
            moments += [square(turn - 1), energy_of(at_points, scaled)]
            fill = jnp.zeros((8 - len(moments), 2 * zone_z), jnp.float32)
            dom_parts[0] = jnp.concatenate(moments + [fill], axis=0)
            dom_copies = [
                send(dom_parts.at[0], dom_parts.at[k], at(k, 0), dom_send.at[k], dom_recv.at[k])
                for k in range(1, n_dom)
            ]
        back = product(plane_value_t[...], split_rows(scaled))
        part[turn] = product(split_lanes(rows_of(back, lanes)), depth_value_t[...]).reshape(
            3, plane, 2 * zone_z
        )
        copies = start_halo(turn)
        if turn < ROUNDS - 1:
            moments += [square(turn - 1), energy_of(at_points, scaled)]
            finish_halo(turn, copies)
    for copy in dom_copies:
        copy.wait_recv()
    sub_parts[0] = jnp.sum(dom_parts[...], axis=0)
    sub_copies = [
        send(sub_parts.at[0], sub_parts.at[k], at(0, k), sub_send.at[k], sub_recv.at[k])
        for k in range(1, n_sub)
    ]
    finish_halo(ROUNDS - 1, copies)
    for copy in sub_copies:
        copy.wait_recv()
    summed = jnp.sum(jnp.sum(sub_parts[...], axis=0), axis=1, keepdims=True)
    mom = [jnp.broadcast_to(summed[k : k + 1], (1, 2 * zone_z)) for k in range(2 * CG_ITERS)]

    def inner(left, right, shift):
        acc = None
        for i, a in enumerate(left):
            for j, b in enumerate(right):
                term = a * b * mom[i + j + shift]
                acc = term if acc is None else acc + term
        return acc

    def combine(left, right, factor):
        out = []
        for k in range(max(len(left), len(right))):
            if k >= len(right):
                out.append(left[k])
            elif k >= len(left):
                out.append(factor * right[k])
            else:
                out.append(left[k] + factor * right[k])
        return out

    one = jnp.ones((1, 2 * zone_z), jnp.float32)
    nil = jnp.zeros((1, 2 * zone_z), jnp.float32)
    answer, rest, direction = [], [one], [one]
    norm = mom[0]
    for sweep in range(CG_ITERS):
        step = norm / inner(direction, direction, 1)
        answer = combine(answer, direction, step)
        rest = combine(rest, [nil] + direction, -step)
        if sweep + 1 < CG_ITERS:
            norm_next = inner(rest, rest, 0)
            direction = combine(rest, direction, norm_next / norm)
            norm = norm_next
    for k, factor in enumerate(answer + rest):
        factors[k] = factor
    for copy in sends:
        copy.wait_send()


def combine_kernel(node_y, pad_y, total, factors, rate, accel, residual, energy_rate, one, two, sem):
    rate_copy = pltpu.make_async_copy(rate, energy_rate, sem.at[0])
    rate_copy.start()
    for k, (spot, out, first, count) in enumerate(
        ((one, accel, 0, CG_ITERS), (two, residual, CG_ITERS, ROUNDS))
    ):
        for x in range(one.shape[0]):
            for c in range(3):
                terms = [
                    factors[first + i] * total[i, c, x * pad_y : x * pad_y + node_y, :]
                    for i in range(count)
                ]
                spot[x, :, c, :] = sum(terms[1:], terms[0])
        pltpu.make_async_copy(spot, out, sem.at[1 + k]).start()
    rate_copy.wait()
    for k, (spot, out) in enumerate(((one, accel), (two, residual))):
        pltpu.make_async_copy(spot, out, sem.at[1 + k]).wait()


def per_device(
    velocity, displacement, energy, rho_weight, mass_share, energy_share, material_id, mix_mask
):
    n_dom, n_sub = lax.axis_size("dom"), lax.axis_size("sub")
    zone_x, zone_y, zone_z = energy.shape[1:]
    node_x, node_y = 2 * zone_x + 1, 2 * zone_y + 1
    pad_x, pad_y = round_up(node_x, 8), round_up(node_y, 8)
    lanes = 4 * zone_z
    plane, wide, tile = node_x * pad_y, 9 * zone_x * zone_y, zone_x * zone_y
    dims = (n_dom, n_sub, zone_x, zone_y, zone_z, pad_x, pad_y, lanes)

    z_value = depth_matrix(value_one, zone_z, lanes)
    z_slope = depth_matrix(slope_one, zone_z, lanes)
    xy = [
        plane_matrix(first, second, zone_x, zone_y, pad_y)
        for first, second in ((value_one, value_one), (slope_one, value_one), (value_one, slope_one))
    ]
    xy_t = [table.T for table in xy]
    weights = np.zeros((9, tile, 4, zone_z), np.float32)
    for a in range(3):
        for b in range(3):
            for q in range(3):
                weights[a * 3 + b, :, q] = quad_one[a] * quad_one[b] * quad_one[q]
    order = (1, 2, 0, 3)
    inputs = (
        jnp.transpose(displacement, order),
        split_table(z_value, 0),
        split_table(z_slope, 0),
        split_table(np.concatenate([xy[1], xy[2]], 0), 1),
        split_table(xy[0], 1),
        material_id,
        mix_mask,
        mass_share,
        energy_share,
        energy,
        rho_weight,
        weights.reshape(wide, lanes),
        split_table(np.concatenate([xy_t[1], xy_t[2]], 1), 1),
        split_table(xy_t[0], 1),
        split_table(np.concatenate([z_value.T, z_slope.T], 0), 0),
        jnp.transpose(velocity, order),
        split_table(z_value.T, 0),
    )
    inputs = [pltpu.with_memory_space_constraint(jnp.asarray(array), pltpu.HBM) for array in inputs]
    f32 = jnp.float32
    vmem = pl.BlockSpec(memory_space=pltpu.VMEM)
    nodes_out = jax.ShapeDtypeStruct((node_x, node_y, 3, 2 * zone_z), f32)
    rate_out = jax.ShapeDtypeStruct(energy.shape, f32)
    total, factors, rate = pl.pallas_call(
        functools.partial(kernel, dims),
        out_shape=(
            jax.ShapeDtypeStruct((ROUNDS, 3, plane, 2 * zone_z), f32),
            jax.ShapeDtypeStruct((CG_ITERS + ROUNDS, 1, 2 * zone_z), f32),
            rate_out,
        ),
        in_specs=[pl.BlockSpec(memory_space=pltpu.HBM)] * N_INPUTS,
        out_specs=(vmem,) * 3,
        scratch_shapes=[pltpu.VMEM(array.shape, array.dtype) for array in inputs]
        + [
            pltpu.SemaphoreType.DMA((N_INPUTS,)),
            pltpu.VMEM((2, 3, plane, 2 * zone_z), f32),
            pltpu.VMEM((wide, lanes), f32),
            pltpu.VMEM((3 * MATS + 8, tile, 2 * zone_z), f32),
            pltpu.VMEM((3, wide, 3 * lanes), f32),
            pltpu.VMEM((3, wide, 3 * lanes), f32),
            pltpu.VMEM((ROUNDS, 3, plane, 2 * zone_z), f32),
            pltpu.VMEM((ROUNDS, 2, node_x, 3, 1, 2 * zone_z), f32),
            pltpu.VMEM((ROUNDS, 4, 3, 1, 2 * zone_z), f32),
            pltpu.VMEM((ROUNDS, 2, 3, pad_y, 2 * zone_z), f32),
            pltpu.VMEM((ROUNDS, 2, node_x, 3, 1, 2 * zone_z), f32),
            pltpu.VMEM((ROUNDS, 4, 3, 1, 2 * zone_z), f32),
            pltpu.VMEM((n_dom, 8, 2 * zone_z), f32),
            pltpu.VMEM((n_sub, 8, 2 * zone_z), f32),
            pltpu.SemaphoreType.DMA((ROUNDS, 8)),
            pltpu.SemaphoreType.DMA((ROUNDS, 8)),
            pltpu.SemaphoreType.DMA((n_dom,)),
            pltpu.SemaphoreType.DMA((n_dom,)),
            pltpu.SemaphoreType.DMA((n_sub,)),
            pltpu.SemaphoreType.DMA((n_sub,)),
        ],
        compiler_params=pltpu.CompilerParams(
            collective_id=0, has_side_effects=True, vmem_limit_bytes=48 * 2**20
        ),
    )(*inputs)
    hbm = pl.BlockSpec(memory_space=pltpu.HBM)
    accel, residual, energy_rate = pl.pallas_call(
        functools.partial(combine_kernel, node_y, pad_y),
        out_shape=(nodes_out, nodes_out, rate_out),
        in_specs=[vmem] * 3,
        out_specs=(hbm,) * 3,
        scratch_shapes=[
            pltpu.VMEM(nodes_out.shape, f32),
            pltpu.VMEM(nodes_out.shape, f32),
            pltpu.SemaphoreType.DMA((3,)),
        ],
        compiler_params=pltpu.CompilerParams(vmem_limit_bytes=8 * 2**20),
    )(total, factors, rate)
    back = (2, 0, 1, 3)
    return jnp.transpose(accel, back), jnp.transpose(residual, back), energy_rate


def solution(mesh):
    blocks = P(None, "dom", "sub", None)
    return jax.shard_map(
        per_device,
        mesh=mesh,
        in_specs=(blocks,) * 6 + (P("dom", "sub", None), blocks),
        out_specs=(blocks,) * 3,
        check_vma=False,
    )
```

```python
import functools
import math

import jax
import jax.numpy as jnp
import numpy as np
from jax import lax
from jax.experimental import pallas as pl
from jax.experimental.pallas import tpu as pltpu
from jax.sharding import PartitionSpec as P
import ml_dtypes

MESH = pl.DeviceIdType.MESH
MATS = 4
EQ_ITERS = 4
CG_ITERS = 3
ROUNDS = CG_ITERS + 1
N_INPUTS = 18

gammas = (1.4, 1.67, 2.0, 3.0)
cold_terms = (0.3, 1.2, 0.6, 2.4)

spread_root = math.sqrt(0.15)
points = np.array([0.5 - spread_root, 0.5, 0.5 + spread_root])
quad_one = np.array([5.0, 8.0, 5.0]) / 18.0
value_one = np.stack(
    [
        2.0 * (points - 0.5) * (points - 1.0),
        -4.0 * points * (points - 1.0),
        2.0 * points * (points - 0.5),
    ],
    1,
)
slope_one = np.stack([4.0 * points - 3.0, 4.0 - 8.0 * points, 4.0 * points - 1.0], 1)
linear_one = np.stack([1.0 - points, points], 1)


def round_up(value, step):
    return -(-value // step) * step


def split_table(table, axis):
    table = table.astype(np.float32)
    high = table.astype(ml_dtypes.bfloat16)
    low = (table - high.astype(np.float32)).astype(ml_dtypes.bfloat16)
    return np.concatenate([high, high, low], axis)


def depth_matrix(one, zone_z, lanes):
    table = np.zeros((2 * zone_z, lanes))
    for q in range(3):
        for z in range(zone_z):
            for k in range(3):
                table[(2 * z + k) % (2 * zone_z), q * zone_z + z] += one[q, k]
    return table


def plane_matrix(one_x, one_y, zone_x, zone_y, pad_y):
    table = np.zeros((9 * zone_x * zone_y, (2 * zone_x + 1) * pad_y))
    for a in range(3):
        for b in range(3):
            for x in range(zone_x):
                for y in range(zone_y):
                    row = ((a * 3 + b) * zone_x + x) * zone_y + y
                    for i in range(3):
                        for j in range(3):
                            table[row, (2 * x + i) * pad_y + 2 * y + j] = one_x[a, i] * one_y[b, j]
    return table


def split_lanes(x):
    high = x.astype(jnp.bfloat16)
    low = (x - high.astype(jnp.float32)).astype(jnp.bfloat16)
    return jnp.concatenate([high, low, high], axis=1)


def split_rows(x):
    high = x.astype(jnp.bfloat16).astype(jnp.float32)
    return jnp.concatenate([high, x - high, high], axis=0).astype(jnp.bfloat16)


def product(left, right):
    return jnp.dot(left, right, preferred_element_type=jnp.float32)


def lanes_of(x, rows):
    return jnp.concatenate([x[c * rows : (c + 1) * rows] for c in range(3)], axis=1)


def rows_of(x, lanes):
    return jnp.concatenate([x[:, c * lanes : (c + 1) * lanes] for c in range(3)], axis=0)


def kernel(
    dims,
    *refs,
):
    outer, refs = refs[:N_INPUTS], refs[N_INPUTS:]
    outputs, refs = refs[:3], refs[3:]
    inner, refs = refs[:N_INPUTS], refs[N_INPUTS:]
    body(dims, outer, *inner, *outputs, *refs)


def body(
    dims,
    outer,
    displacement,
    depth_value,
    depth_slope,
    plane_slopes,
    plane_value,
    material_id,
    mix_mask,
    mass_share,
    energy_share,
    energy,
    rho_weight,
    weight_table,
    plane_slopes_t,
    plane_value_t,
    depth_both_t,
    velocity,
    depth_value_t,
    plane_sides,
    total,
    factors,
    energy_rate,
    load_sem,
    field,
    rows_y,
    rho,
    zone_in,
    jac,
    stress,
    part,
    side_y,
    side_corner,
    face_x,
    face_y,
    corner,
    dom_parts,
    sub_parts,
    halo_send,
    halo_recv,
    dom_send,
    dom_recv,
    sub_send,
    sub_recv,
):
    n_dom, n_sub, zone_x, zone_y, zone_z, pad_x, pad_y, lanes = dims
    node_x, node_y = 2 * zone_x + 1, 2 * zone_y + 1
    plane = node_x * pad_y
    tile = zone_x * zone_y
    wide = 9 * tile
    me_dom, me_sub = lax.axis_index("dom"), lax.axis_index("sub")

    def at(shift_dom, shift_sub):
        return (lax.rem(me_dom + shift_dom + n_dom, n_dom), lax.rem(me_sub + shift_sub + n_sub, n_sub))

    corners = [(-1, -1), (-1, 1), (1, -1), (1, 1)]
    along_dom = [at(k, 0) for k in range(1, n_dom)]
    along_sub = [at(0, k) for k in range(1, n_sub)]
    diagonal = [at(dx, dy) for dx, dy in corners]
    beside_x, beside_y = (along_dom[-1], along_dom[0]), (along_sub[-1], along_sub[0])
    others = along_dom + along_sub + diagonal
    barrier = pltpu.get_barrier_semaphore()
    for other in others:
        pl.semaphore_signal(barrier, inc=1, device_id=other, device_id_type=MESH)

    def gradients(which):
        source = split_lanes(field[which].reshape(3 * plane, 2 * zone_z))
        by_value = split_rows(lanes_of(product(source, depth_value[...]), plane))
        by_slope = split_rows(lanes_of(product(source, depth_slope[...]), plane))
        along_xy = product(plane_slopes[...], by_value)
        along_z = product(plane_value[...], by_slope)
        jac[0] = along_xy[:wide]
        jac[1] = along_xy[wide:]
        jac[2] = along_z

    inner = (
        displacement, depth_value, depth_slope, plane_slopes, plane_value, material_id, mix_mask,
        mass_share, energy_share, energy, rho_weight, weight_table, plane_slopes_t, plane_value_t,
        depth_both_t, velocity, depth_value_t, plane_sides,
    )
    loads = [pltpu.make_async_copy(a, b, load_sem.at[k]) for k, (a, b) in enumerate(zip(outer, inner))]
    for load in loads:
        load.start()
    field[...] = jnp.zeros_like(field)
    rows_y[...] = jnp.zeros_like(rows_y)
    for load in loads[:5]:
        load.wait()

    def unpack(which, source):
        for x in range(node_x):
            for c in range(3):
                field[which, c, x * pad_y : x * pad_y + node_y, :] = source[x, :, c, :]

    unpack(0, displacement)
    gradients(0)
    for load in loads[5:]:
        load.wait()
    for t in range(9):
        for q in range(4):
            for x in range(zone_x):
                rho[t * tile + x * zone_y : t * tile + (x + 1) * zone_y, q * zone_z : (q + 1) * zone_z] = (
                    rho_weight[3 * t + q % 3, x]
                )
    for half in range(2):
        cols = slice(half * zone_z, (half + 1) * zone_z)
        for x in range(zone_x):
            rows = slice(x * zone_y, (x + 1) * zone_y)
            for m in range(MATS):
                present = jnp.where((mix_mask[m, x] == 1) | (material_id[x] == m), 1.0, 0.0)
                zone_in[m, rows, cols] = present
                zone_in[MATS + m, rows, cols] = mass_share[m, x]
                zone_in[2 * MATS + m, rows, cols] = energy_share[m, x]
            for j in range(8):
                zone_in[3 * MATS + j, rows, cols] = energy[j, x]

    present = [zone_in[m] for m in range(MATS)]
    weighted = [present[m] * zone_in[MATS + m] for m in range(MATS)]
    weighted_sum = 1.0 / (weighted[0] + weighted[1] + weighted[2] + weighted[3])
    present_sum = 1.0 / (present[0] + present[1] + present[2] + present[3])

    def spread(x):
        return jnp.concatenate([jnp.concatenate([x, x], axis=1)] * 3, axis=0)

    start = [spread(present[m] * present_sum) for m in range(MATS)]
    load = [
        spread((gammas[m] - 1.0) * (weighted[m] * weighted_sum) * zone_in[2 * MATS + m])
        for m in range(MATS)
    ]
    lane_at = lax.broadcasted_iota(jnp.int32, (tile, lanes), 1) // zone_z
    upper = jnp.where(lane_at == 1, points[1], jnp.where(lane_at == 2, points[2], points[0])).astype(
        jnp.float32
    )
    along = []
    for j in range(4):
        low, high = zone_in[3 * MATS + 2 * j], zone_in[3 * MATS + 2 * j + 1]
        low, high = jnp.concatenate([low, low], axis=1), jnp.concatenate([high, high], axis=1)
        along.append(low + upper * (high - low))

    for a in range(3):
        rows = slice(a * 3 * tile, (a + 1) * 3 * tile)
        x_low = [linear_one[a, 0] * along[jy] + linear_one[a, 1] * along[2 + jy] for jy in range(2)]
        energy_points = jnp.concatenate(
            [linear_one[b, 0] * x_low[0] + linear_one[b, 1] * x_low[1] for b in range(3)], axis=0
        )

        def entry(c, d):
            value = jac[d, rows, c * lanes : (c + 1) * lanes]
            return value + 1.0 if c == d else value

        matrix = [[entry(c, d) for d in range(3)] for c in range(3)]
        adjugate = [[None] * 3 for _ in range(3)]
        for d in range(3):
            for c in range(3):
                adjugate[d][c] = (
                    matrix[(c + 1) % 3][(d + 1) % 3] * matrix[(c + 2) % 3][(d + 2) % 3]
                    - matrix[(c + 1) % 3][(d + 2) % 3] * matrix[(c + 2) % 3][(d + 1) % 3]
                )
        determinant = (
            matrix[0][0] * adjugate[0][0]
            + matrix[0][1] * adjugate[1][0]
            + matrix[0][2] * adjugate[2][0]
        )
        base = rho[rows, :] / determinant * energy_points
        pressure_load = [load[m] * base for m in range(MATS)]
        fraction = list(start)
        for sweep in range(EQ_ITERS):
            grown = []
            for m in range(MATS):
                square = fraction[m] * (pressure_load[m] + cold_terms[m] * fraction[m])
                grown.append(square * lax.rsqrt(jnp.maximum(square, 1e-30)))
            scale = 1.0 / ((grown[0] + grown[1]) + (grown[2] + grown[3]))
            fraction = [grown[m] * scale for m in range(MATS)]
        pressure = (
            (pressure_load[0] + cold_terms[0] * fraction[0])
            + (pressure_load[1] + cold_terms[1] * fraction[1])
            + (pressure_load[2] + cold_terms[2] * fraction[2])
            + (pressure_load[3] + cold_terms[3] * fraction[3])
        )
        weighted_pressure = weight_table[rows, :] * pressure
        for d in range(3):
            for c in range(3):
                stress[d, rows, c * lanes : (c + 1) * lanes] = weighted_pressure * adjugate[d][c]

    sends = []

    def send(source, target, to, send_sem, recv_sem):
        copy = pltpu.make_async_remote_copy(
            src_ref=source,
            dst_ref=target,
            send_sem=send_sem,
            recv_sem=recv_sem,
            device_id=to,
            device_id_type=MESH,
        )
        copy.start()
        sends.append(copy)
        return copy

    last = node_x - 1

    def start_halo(turn):
        for k in range(2):
            row = k * (node_y - 1)
            for x in range(node_x):
                for c in range(3):
                    line = part[turn, c, x * pad_y + row : x * pad_y + row + 1, :]
                    side_y[turn, k, x, c] = line
                    if x == 0:
                        side_corner[turn, k, c] = line
                    if x == last:
                        side_corner[turn, 2 + k, c] = line
        copies = []
        for k, (dx, dy) in enumerate(corners):
            copies.append(
                send(
                    side_corner.at[turn, k],
                    corner.at[turn, k],
                    diagonal[k],
                    halo_send.at[turn, 4 + k],
                    halo_recv.at[turn, 4 + k],
                )
            )
        for k, dy in enumerate((-1, 1)):
            copies.append(
                send(
                    side_y.at[turn, k],
                    face_y.at[turn, k],
                    beside_y[k],
                    halo_send.at[turn, 2 + k],
                    halo_recv.at[turn, 2 + k],
                )
            )
        for k, dx in enumerate((-1, 1)):
            first = 0 if dx < 0 else last * pad_y
            copies.append(
                send(
                    part.at[turn, :, pl.ds(first, pad_y), :],
                    face_x.at[turn, k],
                    beside_x[k],
                    halo_send.at[turn, k],
                    halo_recv.at[turn, k],
                )
            )
        return copies

    def finish_x(turn, copies):
        for copy in copies[6:]:
            copy.wait_recv()
        for x in range(node_x):
            block = part[turn, :, x * pad_y : (x + 1) * pad_y, :]
            if x == 0:
                block = block + face_x[turn, 1]
            if x == last:
                block = block + face_x[turn, 0]
            total[turn, :, x * pad_y : (x + 1) * pad_y, :] = block

    def finish_y(turn, copies):
        for copy in copies[:6]:
            copy.wait_recv()
        for x in range(node_x):
            for c in range(3):
                for k in range(2):
                    line = face_y[turn, 1 - k, x, c]
                    if x == 0:
                        line = line + corner[turn, 3 - k, c]
                    if x == last:
                        line = line + corner[turn, 1 - k, c]
                    rows_y[c, k * pad_x + x : k * pad_x + x + 1, :] = line

    def add_y(turn):
        for x in range(node_x):
            for k in range(2):
                row = x * pad_y + k * (node_y - 1)
                total[turn, :, row : row + 1, :] += rows_y[:, k * pad_x + x : k * pad_x + x + 1, :]

    def owned(turn):
        return [
            total[turn, c, x * pad_y : x * pad_y + 2 * zone_y, :]
            for c in range(3)
            for x in range(2 * zone_x)
        ]

    def tree(terms):
        while len(terms) > 1:
            terms = [sum(terms[k : k + 2]) for k in range(0, len(terms), 2)]
        return jnp.sum(terms[0], axis=0, keepdims=True)

    def square(turn):
        return tree([a * a for a in owned(turn)])

    def energy_of(at_points, scaled):
        both = at_points * scaled
        return tree(
            [
                both[t * tile : (t + 1) * tile, k * 2 * zone_z : (k + 1) * 2 * zone_z]
                for t in range(9)
                for k in range(3 * lanes // (2 * zone_z))
            ]
        )

    side_xy = product(
        plane_slopes_t[...],
        split_rows(jnp.concatenate([stress[0], stress[1]], axis=0)),
    )
    side_z = product(plane_value_t[...], split_rows(stress[2]))
    both = jnp.concatenate([rows_of(side_xy, lanes), rows_of(side_z, lanes)], axis=1)
    part[0] = product(split_lanes(both), depth_both_t[...]).reshape(3, plane, 2 * zone_z)
    pl.semaphore_wait(barrier, len(others))
    copies = start_halo(0)

    mass_weight = weight_table[...] * rho[...]
    unpack(1, velocity)
    gradients(1)
    work = jnp.zeros((wide, lanes), jnp.float32)
    for c in range(3):
        for d in range(3):
            work = work + jac[d, :, c * lanes : (c + 1) * lanes] * stress[d, :, c * lanes : (c + 1) * lanes]

    def to_linear(x):
        results = []
        for jx in range(2):
            for jy in range(2):
                acc = jnp.zeros((tile, lanes), jnp.float32)
                for a in range(3):
                    for b in range(3):
                        t = a * 3 + b
                        acc = acc + float(linear_one[a, jx] * linear_one[b, jy]) * x[t * tile : (t + 1) * tile]
                for jz in range(2):
                    scaled = acc * (upper if jz else 1.0 - upper)
                    folded = scaled[:, : 2 * zone_z] + scaled[:, 2 * zone_z :]
                    results.append(folded + pltpu.roll(folded, zone_z, 1))
        return results

    rates = to_linear(work)
    lumped = to_linear(mass_weight)
    for j in range(8):
        rate = -rates[j] / lumped[j]
        for x in range(zone_x):
            energy_rate[j, x] = rate[x * zone_y : (x + 1) * zone_y, :zone_z]

    moments = []
    weight_three = jnp.concatenate([mass_weight] * 3, axis=1)
    for turn in range(1, ROUNDS):
        finish_x(turn - 1, copies)
        source = split_lanes(total[turn - 1].reshape(3 * plane, 2 * zone_z))
        nodes = split_rows(lanes_of(product(source, depth_value[...]), plane))
        at_points = product(plane_value[...], nodes)
        finish_y(turn - 1, copies)
        source = split_lanes(rows_y[...].reshape(6 * pad_x, 2 * zone_z))
        nodes = split_rows(lanes_of(product(source, depth_value[...]), 2 * pad_x))
        at_points = at_points + product(plane_sides[...], nodes)
        scaled = at_points * weight_three
        if turn == ROUNDS - 1:
            add_y(turn - 1)
            moments += [square(turn - 1), energy_of(at_points, scaled)]
            fill = jnp.zeros((8 - len(moments), 2 * zone_z), jnp.float32)
            dom_parts[0] = jnp.concatenate(moments + [fill], axis=0)
            dom_copies = [
                send(dom_parts.at[0], dom_parts.at[k], along_dom[k - 1], dom_send.at[k], dom_recv.at[k])
                for k in range(1, n_dom)
            ]
        back = product(plane_value_t[...], split_rows(scaled))
        part[turn] = product(split_lanes(rows_of(back, lanes)), depth_value_t[...]).reshape(
            3, plane, 2 * zone_z
        )
        copies = start_halo(turn)
        if turn < ROUNDS - 1:
            add_y(turn - 1)
            moments += [square(turn - 1), energy_of(at_points, scaled)]
    for copy in dom_copies:
        copy.wait_recv()
    sub_parts[0] = jnp.sum(dom_parts[...], axis=0)
    sub_copies = [
        send(sub_parts.at[0], sub_parts.at[k], along_sub[k - 1], sub_send.at[k], sub_recv.at[k])
        for k in range(1, n_sub)
    ]
    finish_x(ROUNDS - 1, copies)
    finish_y(ROUNDS - 1, copies)
    add_y(ROUNDS - 1)
    for copy in sub_copies:
        copy.wait_recv()
    summed = jnp.sum(jnp.sum(sub_parts[...], axis=0), axis=1, keepdims=True)
    mom = [jnp.broadcast_to(summed[k : k + 1], (1, 2 * zone_z)) for k in range(2 * CG_ITERS)]

    def inner(left, right, shift):
        acc = None
        for i, a in enumerate(left):
            for j, b in enumerate(right):
                term = a * b * mom[i + j + shift]
                acc = term if acc is None else acc + term
        return acc

    def combine(left, right, factor):
        out = []
        for k in range(max(len(left), len(right))):
            if k >= len(right):
                out.append(left[k])
            elif k >= len(left):
                out.append(factor * right[k])
            else:
                out.append(left[k] + factor * right[k])
        return out

    one = jnp.ones((1, 2 * zone_z), jnp.float32)
    nil = jnp.zeros((1, 2 * zone_z), jnp.float32)
    answer, rest, direction = [], [one], [one]
    norm = mom[0]
    for sweep in range(CG_ITERS):
        step = norm / inner(direction, direction, 1)
        answer = combine(answer, direction, step)
        rest = combine(rest, [nil] + direction, -step)
        if sweep + 1 < CG_ITERS:
            norm_next = inner(rest, rest, 0)
            direction = combine(rest, direction, norm_next / norm)
            norm = norm_next
    for k, factor in enumerate(answer + rest):
        factors[k] = factor
    for copy in sends:
        copy.wait_send()


def combine_kernel(node_y, pad_y, total, factors, rate, accel, residual, energy_rate, one, two, sem):
    rate_copy = pltpu.make_async_copy(rate, energy_rate, sem.at[0])
    rate_copy.start()
    for k, (spot, out, first, count) in enumerate(
        ((one, accel, 0, CG_ITERS), (two, residual, CG_ITERS, ROUNDS))
    ):
        for x in range(one.shape[0]):
            for c in range(3):
                terms = [
                    factors[first + i] * total[i, c, x * pad_y : x * pad_y + node_y, :]
                    for i in range(count)
                ]
                spot[x, :, c, :] = sum(terms[1:], terms[0])
        pltpu.make_async_copy(spot, out, sem.at[1 + k]).start()
    rate_copy.wait()
    for k, (spot, out) in enumerate(((one, accel), (two, residual))):
        pltpu.make_async_copy(spot, out, sem.at[1 + k]).wait()


def per_device(
    velocity, displacement, energy, rho_weight, mass_share, energy_share, material_id, mix_mask
):
    n_dom, n_sub = lax.axis_size("dom"), lax.axis_size("sub")
    zone_x, zone_y, zone_z = energy.shape[1:]
    node_x, node_y = 2 * zone_x + 1, 2 * zone_y + 1
    pad_x, pad_y = round_up(node_x, 8), round_up(node_y, 8)
    lanes = 4 * zone_z
    plane, wide, tile = node_x * pad_y, 9 * zone_x * zone_y, zone_x * zone_y
    dims = (n_dom, n_sub, zone_x, zone_y, zone_z, pad_x, pad_y, lanes)

    z_value = depth_matrix(value_one, zone_z, lanes)
    z_slope = depth_matrix(slope_one, zone_z, lanes)
    xy = [
        plane_matrix(first, second, zone_x, zone_y, pad_y)
        for first, second in ((value_one, value_one), (slope_one, value_one), (value_one, slope_one))
    ]
    xy_t = [table.T for table in xy]
    sides = np.zeros((wide, 2 * pad_x))
    for x in range(node_x):
        sides[:, x] = xy[0][:, x * pad_y]
        sides[:, pad_x + x] = xy[0][:, x * pad_y + 2 * zone_y]
    weights = np.zeros((9, tile, 4, zone_z), np.float32)
    for a in range(3):
        for b in range(3):
            for q in range(3):
                weights[a * 3 + b, :, q] = quad_one[a] * quad_one[b] * quad_one[q]
    order = (1, 2, 0, 3)
    inputs = (
        jnp.transpose(displacement, order),
        split_table(z_value, 0),
        split_table(z_slope, 0),
        split_table(np.concatenate([xy[1], xy[2]], 0), 1),
        split_table(xy[0], 1),
        material_id,
        mix_mask,
        mass_share,
        energy_share,
        energy,
        rho_weight,
        weights.reshape(wide, lanes),
        split_table(np.concatenate([xy_t[1], xy_t[2]], 1), 1),
        split_table(xy_t[0], 1),
        split_table(np.concatenate([z_value.T, z_slope.T], 0), 0),
        jnp.transpose(velocity, order),
        split_table(z_value.T, 0),
        split_table(sides, 1),
    )
    inputs = [pltpu.with_memory_space_constraint(jnp.asarray(array), pltpu.HBM) for array in inputs]
    f32 = jnp.float32
    vmem = pl.BlockSpec(memory_space=pltpu.VMEM)
    nodes_out = jax.ShapeDtypeStruct((node_x, node_y, 3, 2 * zone_z), f32)
    rate_out = jax.ShapeDtypeStruct(energy.shape, f32)
    total, factors, rate = pl.pallas_call(
        functools.partial(kernel, dims),
        out_shape=(
            jax.ShapeDtypeStruct((ROUNDS, 3, plane, 2 * zone_z), f32),
            jax.ShapeDtypeStruct((CG_ITERS + ROUNDS, 1, 2 * zone_z), f32),
            rate_out,
        ),
        in_specs=[pl.BlockSpec(memory_space=pltpu.HBM)] * N_INPUTS,
        out_specs=(vmem,) * 3,
        scratch_shapes=[pltpu.VMEM(array.shape, array.dtype) for array in inputs]
        + [
            pltpu.SemaphoreType.DMA((N_INPUTS,)),
            pltpu.VMEM((2, 3, plane, 2 * zone_z), f32),
            pltpu.VMEM((3, 2 * pad_x, 2 * zone_z), f32),
            pltpu.VMEM((wide, lanes), f32),
            pltpu.VMEM((3 * MATS + 8, tile, 2 * zone_z), f32),
            pltpu.VMEM((3, wide, 3 * lanes), f32),
            pltpu.VMEM((3, wide, 3 * lanes), f32),
            pltpu.VMEM((ROUNDS, 3, plane, 2 * zone_z), f32),
            pltpu.VMEM((ROUNDS, 2, node_x, 3, 1, 2 * zone_z), f32),
            pltpu.VMEM((ROUNDS, 4, 3, 1, 2 * zone_z), f32),
            pltpu.VMEM((ROUNDS, 2, 3, pad_y, 2 * zone_z), f32),
            pltpu.VMEM((ROUNDS, 2, node_x, 3, 1, 2 * zone_z), f32),
            pltpu.VMEM((ROUNDS, 4, 3, 1, 2 * zone_z), f32),
            pltpu.VMEM((n_dom, 8, 2 * zone_z), f32),
            pltpu.VMEM((n_sub, 8, 2 * zone_z), f32),
            pltpu.SemaphoreType.DMA((ROUNDS, 8)),
            pltpu.SemaphoreType.DMA((ROUNDS, 8)),
            pltpu.SemaphoreType.DMA((n_dom,)),
            pltpu.SemaphoreType.DMA((n_dom,)),
            pltpu.SemaphoreType.DMA((n_sub,)),
            pltpu.SemaphoreType.DMA((n_sub,)),
        ],
        compiler_params=pltpu.CompilerParams(
            collective_id=0, has_side_effects=True, vmem_limit_bytes=48 * 2**20
        ),
    )(*inputs)
    hbm = pl.BlockSpec(memory_space=pltpu.HBM)
    accel, residual, energy_rate = pl.pallas_call(
        functools.partial(combine_kernel, node_y, pad_y),
        out_shape=(nodes_out, nodes_out, rate_out),
        in_specs=[vmem] * 3,
        out_specs=(hbm,) * 3,
        scratch_shapes=[
            pltpu.VMEM(nodes_out.shape, f32),
            pltpu.VMEM(nodes_out.shape, f32),
            pltpu.SemaphoreType.DMA((3,)),
        ],
        compiler_params=pltpu.CompilerParams(vmem_limit_bytes=8 * 2**20),
    )(total, factors, rate)
    back = (2, 0, 1, 3)
    return jnp.transpose(accel, back), jnp.transpose(residual, back), energy_rate


def solution(mesh):
    blocks = P(None, "dom", "sub", None)
    return jax.shard_map(
        per_device,
        mesh=mesh,
        in_specs=(blocks,) * 6 + (P("dom", "sub", None), blocks),
        out_specs=(blocks,) * 3,
        check_vma=False,
    )
```

```python
import functools
import math

import jax
import jax.numpy as jnp
import numpy as np
from jax import lax
from jax.experimental import pallas as pl
from jax.experimental.pallas import tpu as pltpu
from jax.sharding import PartitionSpec as P
import ml_dtypes

MESH = pl.DeviceIdType.MESH
MATS = 4
EQ_ITERS = 4
CG_ITERS = 3
ROUNDS = CG_ITERS + 1
N_INPUTS = 18

gammas = (1.4, 1.67, 2.0, 3.0)
cold_terms = (0.3, 1.2, 0.6, 2.4)

spread_root = math.sqrt(0.15)
points = np.array([0.5 - spread_root, 0.5, 0.5 + spread_root])
quad_one = np.array([5.0, 8.0, 5.0]) / 18.0
value_one = np.stack(
    [
        2.0 * (points - 0.5) * (points - 1.0),
        -4.0 * points * (points - 1.0),
        2.0 * points * (points - 0.5),
    ],
    1,
)
slope_one = np.stack([4.0 * points - 3.0, 4.0 - 8.0 * points, 4.0 * points - 1.0], 1)
linear_one = np.stack([1.0 - points, points], 1)


def round_up(value, step):
    return -(-value // step) * step


def split_table(table, axis):
    table = table.astype(np.float32)
    high = table.astype(ml_dtypes.bfloat16)
    low = (table - high.astype(np.float32)).astype(ml_dtypes.bfloat16)
    return np.concatenate([high, high, low], axis)


def depth_matrix(one, zone_z, lanes):
    table = np.zeros((2 * zone_z, lanes))
    for q in range(3):
        for z in range(zone_z):
            for k in range(3):
                table[(2 * z + k) % (2 * zone_z), q * zone_z + z] += one[q, k]
    return table


def plane_matrix(one_x, one_y, zone_x, zone_y, pad_y):
    table = np.zeros((9 * zone_x * zone_y, (2 * zone_x + 1) * pad_y))
    for a in range(3):
        for b in range(3):
            for x in range(zone_x):
                for y in range(zone_y):
                    row = ((a * 3 + b) * zone_x + x) * zone_y + y
                    for i in range(3):
                        for j in range(3):
                            table[row, (2 * x + i) * pad_y + 2 * y + j] = one_x[a, i] * one_y[b, j]
    return table


def split_lanes(x):
    high = x.astype(jnp.bfloat16)
    low = (x - high.astype(jnp.float32)).astype(jnp.bfloat16)
    return jnp.concatenate([high, low, high], axis=1)


def split_rows(x):
    high = x.astype(jnp.bfloat16).astype(jnp.float32)
    return jnp.concatenate([high, x - high, high], axis=0).astype(jnp.bfloat16)


def product(left, right):
    return jnp.dot(left, right, preferred_element_type=jnp.float32)


def lanes_of(x, rows):
    return jnp.concatenate([x[c * rows : (c + 1) * rows] for c in range(3)], axis=1)


def rows_of(x, lanes):
    return jnp.concatenate([x[:, c * lanes : (c + 1) * lanes] for c in range(3)], axis=0)


def kernel(
    dims,
    *refs,
):
    outer, refs = refs[:N_INPUTS], refs[N_INPUTS:]
    outputs, refs = refs[:3], refs[3:]
    inner, refs = refs[:N_INPUTS], refs[N_INPUTS:]
    body(dims, outer, *inner, *outputs, *refs)


def body(
    dims,
    outer,
    displacement,
    depth_value,
    depth_slope,
    plane_slopes,
    plane_value,
    material_id,
    mix_mask,
    mass_share,
    energy_share,
    energy,
    rho_weight,
    weight_table,
    plane_slopes_t,
    plane_value_t,
    depth_both_t,
    velocity,
    depth_value_t,
    plane_sides,
    total,
    factors,
    energy_rate,
    load_sem,
    field,
    rows_y,
    rho,
    zone_in,
    jac,
    stress,
    part,
    side_y,
    side_corner,
    face_x,
    face_y,
    corner,
    dom_parts,
    sub_parts,
    halo_send,
    halo_recv,
    dom_send,
    dom_recv,
    sub_send,
    sub_recv,
):
    n_dom, n_sub, zone_x, zone_y, zone_z, pad_x, pad_y, lanes = dims
    node_x, node_y = 2 * zone_x + 1, 2 * zone_y + 1
    plane = node_x * pad_y
    tile = zone_x * zone_y
    wide = 9 * tile
    me_dom, me_sub = lax.axis_index("dom"), lax.axis_index("sub")

    def at(shift_dom, shift_sub):
        return (lax.rem(me_dom + shift_dom + n_dom, n_dom), lax.rem(me_sub + shift_sub + n_sub, n_sub))

    corners = [(-1, -1), (-1, 1), (1, -1), (1, 1)]
    along_dom = [at(k, 0) for k in range(1, n_dom)]
    along_sub = [at(0, k) for k in range(1, n_sub)]
    diagonal = [at(dx, dy) for dx, dy in corners]
    beside_x, beside_y = (along_dom[-1], along_dom[0]), (along_sub[-1], along_sub[0])
    others = along_dom + along_sub + diagonal
    barrier = pltpu.get_barrier_semaphore()
    for other in others:
        pl.semaphore_signal(barrier, inc=1, device_id=other, device_id_type=MESH)

    def gradients(which):
        source = split_lanes(field[which].reshape(3 * plane, 2 * zone_z))
        by_value = split_rows(lanes_of(product(source, depth_value[...]), plane))
        by_slope = split_rows(lanes_of(product(source, depth_slope[...]), plane))
        along_xy = product(plane_slopes[...], by_value)
        along_z = product(plane_value[...], by_slope)
        jac[0] = along_xy[:wide]
        jac[1] = along_xy[wide:]
        jac[2] = along_z

    inner = (
        displacement, depth_value, depth_slope, plane_slopes, plane_value, material_id, mix_mask,
        mass_share, energy_share, energy, rho_weight, weight_table, plane_slopes_t, plane_value_t,
        depth_both_t, velocity, depth_value_t, plane_sides,
    )
    loads = [pltpu.make_async_copy(a, b, load_sem.at[k]) for k, (a, b) in enumerate(zip(outer, inner))]
    for load in loads:
        load.start()
    field[...] = jnp.zeros_like(field)
    rows_y[...] = jnp.zeros_like(rows_y)
    for load in loads[:5]:
        load.wait()

    def unpack(which, source):
        for x in range(node_x):
            for c in range(3):
                field[which, c, x * pad_y : x * pad_y + node_y, :] = source[x, :, c, :]

    unpack(0, displacement)
    gradients(0)
    for load in loads[5:]:
        load.wait()
    for t in range(9):
        for q in range(4):
            for x in range(zone_x):
                rho[t * tile + x * zone_y : t * tile + (x + 1) * zone_y, q * zone_z : (q + 1) * zone_z] = (
                    rho_weight[3 * t + q % 3, x]
                )
    for half in range(2):
        cols = slice(half * zone_z, (half + 1) * zone_z)
        for x in range(zone_x):
            rows = slice(x * zone_y, (x + 1) * zone_y)
            for m in range(MATS):
                present = jnp.where((mix_mask[m, x] == 1) | (material_id[x] == m), 1.0, 0.0)
                zone_in[m, rows, cols] = present
                zone_in[MATS + m, rows, cols] = mass_share[m, x]
                zone_in[2 * MATS + m, rows, cols] = energy_share[m, x]
            for j in range(8):
                zone_in[3 * MATS + j, rows, cols] = energy[j, x]

    present = [zone_in[m] for m in range(MATS)]
    weighted = [present[m] * zone_in[MATS + m] for m in range(MATS)]
    weighted_sum = 1.0 / (weighted[0] + weighted[1] + weighted[2] + weighted[3])
    present_sum = 1.0 / (present[0] + present[1] + present[2] + present[3])

    def spread(x):
        return jnp.concatenate([jnp.concatenate([x, x], axis=1)] * 3, axis=0)

    start = [spread(present[m] * present_sum) for m in range(MATS)]
    load = [
        spread((gammas[m] - 1.0) * (weighted[m] * weighted_sum) * zone_in[2 * MATS + m])
        for m in range(MATS)
    ]
    lane_at = lax.broadcasted_iota(jnp.int32, (tile, lanes), 1) // zone_z
    upper = jnp.where(lane_at == 1, points[1], jnp.where(lane_at == 2, points[2], points[0])).astype(
        jnp.float32
    )
    along = []
    for j in range(4):
        low, high = zone_in[3 * MATS + 2 * j], zone_in[3 * MATS + 2 * j + 1]
        low, high = jnp.concatenate([low, low], axis=1), jnp.concatenate([high, high], axis=1)
        along.append(low + upper * (high - low))

    for a in range(3):
        rows = slice(a * 3 * tile, (a + 1) * 3 * tile)
        x_low = [linear_one[a, 0] * along[jy] + linear_one[a, 1] * along[2 + jy] for jy in range(2)]
        energy_points = jnp.concatenate(
            [linear_one[b, 0] * x_low[0] + linear_one[b, 1] * x_low[1] for b in range(3)], axis=0
        )

        def entry(c, d):
            value = jac[d, rows, c * lanes : (c + 1) * lanes]
            return value + 1.0 if c == d else value

        matrix = [[entry(c, d) for d in range(3)] for c in range(3)]
        adjugate = [[None] * 3 for _ in range(3)]
        for d in range(3):
            for c in range(3):
                adjugate[d][c] = (
                    matrix[(c + 1) % 3][(d + 1) % 3] * matrix[(c + 2) % 3][(d + 2) % 3]
                    - matrix[(c + 1) % 3][(d + 2) % 3] * matrix[(c + 2) % 3][(d + 1) % 3]
                )
        determinant = (
            matrix[0][0] * adjugate[0][0]
            + matrix[0][1] * adjugate[1][0]
            + matrix[0][2] * adjugate[2][0]
        )
        base = rho[rows, :] / determinant * energy_points
        pressure_load = [load[m] * base for m in range(MATS)]
        fraction = list(start)
        for sweep in range(EQ_ITERS):
            grown = []
            for m in range(MATS):
                square = fraction[m] * (pressure_load[m] + cold_terms[m] * fraction[m])
                grown.append(square * lax.rsqrt(jnp.maximum(square, 1e-30)))
            scale = 1.0 / ((grown[0] + grown[1]) + (grown[2] + grown[3]))
            fraction = [grown[m] * scale for m in range(MATS)]
        pressure = (
            (pressure_load[0] + cold_terms[0] * fraction[0])
            + (pressure_load[1] + cold_terms[1] * fraction[1])
            + (pressure_load[2] + cold_terms[2] * fraction[2])
            + (pressure_load[3] + cold_terms[3] * fraction[3])
        )
        weighted_pressure = weight_table[rows, :] * pressure
        for d in range(3):
            for c in range(3):
                stress[d, rows, c * lanes : (c + 1) * lanes] = weighted_pressure * adjugate[d][c]

    sends = []

    def send(source, target, to, send_sem, recv_sem):
        copy = pltpu.make_async_remote_copy(
            src_ref=source,
            dst_ref=target,
            send_sem=send_sem,
            recv_sem=recv_sem,
            device_id=to,
            device_id_type=MESH,
        )
        copy.start()
        sends.append(copy)
        return copy

    last = node_x - 1

    def start_halo(turn):
        for k in range(2):
            row = k * (node_y - 1)
            for x in range(node_x):
                for c in range(3):
                    line = part[turn, c, x * pad_y + row : x * pad_y + row + 1, :]
                    side_y[turn, k, x, c] = line
                    if x == 0:
                        side_corner[turn, k, c] = line
                    if x == last:
                        side_corner[turn, 2 + k, c] = line
        copies = []
        for k, (dx, dy) in enumerate(corners):
            copies.append(
                send(
                    side_corner.at[turn, k],
                    corner.at[turn, k],
                    diagonal[k],
                    halo_send.at[turn, 4 + k],
                    halo_recv.at[turn, 4 + k],
                )
            )
        for k, dy in enumerate((-1, 1)):
            copies.append(
                send(
                    side_y.at[turn, k],
                    face_y.at[turn, k],
                    beside_y[k],
                    halo_send.at[turn, 2 + k],
                    halo_recv.at[turn, 2 + k],
                )
            )
        for k, dx in enumerate((-1, 1)):
            first = 0 if dx < 0 else last * pad_y
            copies.append(
                send(
                    part.at[turn, :, pl.ds(first, pad_y), :],
                    face_x.at[turn, k],
                    beside_x[k],
                    halo_send.at[turn, k],
                    halo_recv.at[turn, k],
                )
            )
        return copies

    def finish_x(turn, copies):
        for copy in copies[6:]:
            copy.wait_recv()
        for x in range(node_x):
            block = part[turn, :, x * pad_y : (x + 1) * pad_y, :]
            if x == 0:
                block = block + face_x[turn, 1]
            if x == last:
                block = block + face_x[turn, 0]
            total[turn, :, x * pad_y : (x + 1) * pad_y, :] = block

    def finish_y(turn, copies):
        for copy in copies[:6]:
            copy.wait_recv()
        for x in range(node_x):
            for c in range(3):
                for k in range(2):
                    line = face_y[turn, 1 - k, x, c]
                    if x == 0:
                        line = line + corner[turn, 3 - k, c]
                    if x == last:
                        line = line + corner[turn, 1 - k, c]
                    rows_y[c, k * pad_x + x : k * pad_x + x + 1, :] = line

    def add_y(turn):
        for x in range(node_x):
            for k in range(2):
                row = x * pad_y + k * (node_y - 1)
                total[turn, :, row : row + 1, :] += rows_y[:, k * pad_x + x : k * pad_x + x + 1, :]

    def owned(turn):
        return [
            total[turn, c, x * pad_y : x * pad_y + 2 * zone_y, :]
            for c in range(3)
            for x in range(2 * zone_x)
        ]

    def tree(terms):
        while len(terms) > 1:
            terms = [sum(terms[k : k + 2]) for k in range(0, len(terms), 2)]
        return jnp.sum(terms[0], axis=0, keepdims=True)

    def square(turn):
        return tree([a * a for a in owned(turn)])

    def energy_of(at_points, scaled):
        both = at_points * scaled
        return tree(
            [
                both[t * tile : (t + 1) * tile, k * 2 * zone_z : (k + 1) * 2 * zone_z]
                for t in range(9)
                for k in range(3 * lanes // (2 * zone_z))
            ]
        )

    side_xy = product(
        plane_slopes_t[...],
        split_rows(jnp.concatenate([stress[0], stress[1]], axis=0)),
    )
    side_z = product(plane_value_t[...], split_rows(stress[2]))
    both = jnp.concatenate([rows_of(side_xy, lanes), rows_of(side_z, lanes)], axis=1)
    part[0] = product(split_lanes(both), depth_both_t[...]).reshape(3, plane, 2 * zone_z)
    pl.semaphore_wait(barrier, len(others))
    copies = start_halo(0)

    mass_weight = weight_table[...] * rho[...]

    def contract():
        work = jnp.zeros((wide, lanes), jnp.float32)
        for c in range(3):
            for d in range(3):
                cols = slice(c * lanes, (c + 1) * lanes)
                work = work + jac[d, :, cols] * stress[d, :, cols]
        return work

    def to_linear(x):
        results = []
        for jx in range(2):
            for jy in range(2):
                acc = jnp.zeros((tile, lanes), jnp.float32)
                for a in range(3):
                    for b in range(3):
                        t = a * 3 + b
                        acc = acc + float(linear_one[a, jx] * linear_one[b, jy]) * x[t * tile : (t + 1) * tile]
                for jz in range(2):
                    scaled = acc * (upper if jz else 1.0 - upper)
                    folded = scaled[:, : 2 * zone_z] + scaled[:, 2 * zone_z :]
                    results.append(folded + pltpu.roll(folded, zone_z, 1))
        return results

    def store_rate():
        rates = to_linear(contract())
        lumped = to_linear(mass_weight)
        for j in range(8):
            rate = -rates[j] / lumped[j]
            for x in range(zone_x):
                energy_rate[j, x] = rate[x * zone_y : (x + 1) * zone_y, :zone_z]

    moments = []
    weight_three = jnp.concatenate([mass_weight] * 3, axis=1)
    for turn in range(1, ROUNDS):
        finish_x(turn - 1, copies)
        source = split_lanes(total[turn - 1].reshape(3 * plane, 2 * zone_z))
        nodes = split_rows(lanes_of(product(source, depth_value[...]), plane))
        at_points = product(plane_value[...], nodes)
        finish_y(turn - 1, copies)
        source = split_lanes(rows_y[...].reshape(6 * pad_x, 2 * zone_z))
        nodes = split_rows(lanes_of(product(source, depth_value[...]), 2 * pad_x))
        at_points = at_points + product(plane_sides[...], nodes)
        scaled = at_points * weight_three
        if turn == ROUNDS - 1:
            add_y(turn - 1)
            moments += [square(turn - 1), energy_of(at_points, scaled)]
            fill = jnp.zeros((8 - len(moments), 2 * zone_z), jnp.float32)
            dom_parts[0] = jnp.concatenate(moments + [fill], axis=0)
            dom_copies = [
                send(dom_parts.at[0], dom_parts.at[k], along_dom[k - 1], dom_send.at[k], dom_recv.at[k])
                for k in range(1, n_dom)
            ]
        back = product(plane_value_t[...], split_rows(scaled))
        part[turn] = product(split_lanes(rows_of(back, lanes)), depth_value_t[...]).reshape(
            3, plane, 2 * zone_z
        )
        copies = start_halo(turn)
        if turn < ROUNDS - 1:
            add_y(turn - 1)
            moments += [square(turn - 1), energy_of(at_points, scaled)]
        if turn == 1:
            unpack(1, velocity)
            gradients(1)
        if turn == 2:
            store_rate()
    for copy in dom_copies:
        copy.wait_recv()
    sub_parts[0] = jnp.sum(dom_parts[...], axis=0)
    sub_copies = [
        send(sub_parts.at[0], sub_parts.at[k], along_sub[k - 1], sub_send.at[k], sub_recv.at[k])
        for k in range(1, n_sub)
    ]
    finish_x(ROUNDS - 1, copies)
    finish_y(ROUNDS - 1, copies)
    add_y(ROUNDS - 1)
    for copy in sub_copies:
        copy.wait_recv()
    summed = jnp.sum(jnp.sum(sub_parts[...], axis=0), axis=1, keepdims=True)
    mom = [jnp.broadcast_to(summed[k : k + 1], (1, 2 * zone_z)) for k in range(2 * CG_ITERS)]

    def inner(left, right, shift):
        acc = None
        for i, a in enumerate(left):
            for j, b in enumerate(right):
                term = a * b * mom[i + j + shift]
                acc = term if acc is None else acc + term
        return acc

    def combine(left, right, factor):
        out = []
        for k in range(max(len(left), len(right))):
            if k >= len(right):
                out.append(left[k])
            elif k >= len(left):
                out.append(factor * right[k])
            else:
                out.append(left[k] + factor * right[k])
        return out

    one = jnp.ones((1, 2 * zone_z), jnp.float32)
    nil = jnp.zeros((1, 2 * zone_z), jnp.float32)
    answer, rest, direction = [], [one], [one]
    norm = mom[0]
    for sweep in range(CG_ITERS):
        step = norm / inner(direction, direction, 1)
        answer = combine(answer, direction, step)
        rest = combine(rest, [nil] + direction, -step)
        if sweep + 1 < CG_ITERS:
            norm_next = inner(rest, rest, 0)
            direction = combine(rest, direction, norm_next / norm)
            norm = norm_next
    for k, factor in enumerate(answer + rest):
        factors[k] = factor
    for copy in sends:
        copy.wait_send()


def combine_kernel(node_y, pad_y, total, factors, rate, accel, residual, energy_rate, one, two, sem):
    rate_copy = pltpu.make_async_copy(rate, energy_rate, sem.at[0])
    rate_copy.start()
    for k, (spot, out, first, count) in enumerate(
        ((one, accel, 0, CG_ITERS), (two, residual, CG_ITERS, ROUNDS))
    ):
        for x in range(one.shape[0]):
            for c in range(3):
                terms = [
                    factors[first + i] * total[i, c, x * pad_y : x * pad_y + node_y, :]
                    for i in range(count)
                ]
                spot[x, :, c, :] = sum(terms[1:], terms[0])
        pltpu.make_async_copy(spot, out, sem.at[1 + k]).start()
    rate_copy.wait()
    for k, (spot, out) in enumerate(((one, accel), (two, residual))):
        pltpu.make_async_copy(spot, out, sem.at[1 + k]).wait()


def per_device(
    velocity, displacement, energy, rho_weight, mass_share, energy_share, material_id, mix_mask
):
    n_dom, n_sub = lax.axis_size("dom"), lax.axis_size("sub")
    zone_x, zone_y, zone_z = energy.shape[1:]
    node_x, node_y = 2 * zone_x + 1, 2 * zone_y + 1
    pad_x, pad_y = round_up(node_x, 8), round_up(node_y, 8)
    lanes = 4 * zone_z
    plane, wide, tile = node_x * pad_y, 9 * zone_x * zone_y, zone_x * zone_y
    dims = (n_dom, n_sub, zone_x, zone_y, zone_z, pad_x, pad_y, lanes)

    z_value = depth_matrix(value_one, zone_z, lanes)
    z_slope = depth_matrix(slope_one, zone_z, lanes)
    xy = [
        plane_matrix(first, second, zone_x, zone_y, pad_y)
        for first, second in ((value_one, value_one), (slope_one, value_one), (value_one, slope_one))
    ]
    xy_t = [table.T for table in xy]
    sides = np.zeros((wide, 2 * pad_x))
    for x in range(node_x):
        sides[:, x] = xy[0][:, x * pad_y]
        sides[:, pad_x + x] = xy[0][:, x * pad_y + 2 * zone_y]
    weights = np.zeros((9, tile, 4, zone_z), np.float32)
    for a in range(3):
        for b in range(3):
            for q in range(3):
                weights[a * 3 + b, :, q] = quad_one[a] * quad_one[b] * quad_one[q]
    order = (1, 2, 0, 3)
    inputs = (
        jnp.transpose(displacement, order),
        split_table(z_value, 0),
        split_table(z_slope, 0),
        split_table(np.concatenate([xy[1], xy[2]], 0), 1),
        split_table(xy[0], 1),
        material_id,
        mix_mask,
        mass_share,
        energy_share,
        energy,
        rho_weight,
        weights.reshape(wide, lanes),
        split_table(np.concatenate([xy_t[1], xy_t[2]], 1), 1),
        split_table(xy_t[0], 1),
        split_table(np.concatenate([z_value.T, z_slope.T], 0), 0),
        jnp.transpose(velocity, order),
        split_table(z_value.T, 0),
        split_table(sides, 1),
    )
    inputs = [pltpu.with_memory_space_constraint(jnp.asarray(array), pltpu.HBM) for array in inputs]
    f32 = jnp.float32
    vmem = pl.BlockSpec(memory_space=pltpu.VMEM)
    nodes_out = jax.ShapeDtypeStruct((node_x, node_y, 3, 2 * zone_z), f32)
    rate_out = jax.ShapeDtypeStruct(energy.shape, f32)
    total, factors, rate = pl.pallas_call(
        functools.partial(kernel, dims),
        out_shape=(
            jax.ShapeDtypeStruct((ROUNDS, 3, plane, 2 * zone_z), f32),
            jax.ShapeDtypeStruct((CG_ITERS + ROUNDS, 1, 2 * zone_z), f32),
            rate_out,
        ),
        in_specs=[pl.BlockSpec(memory_space=pltpu.HBM)] * N_INPUTS,
        out_specs=(vmem,) * 3,
        scratch_shapes=[pltpu.VMEM(array.shape, array.dtype) for array in inputs]
        + [
            pltpu.SemaphoreType.DMA((N_INPUTS,)),
            pltpu.VMEM((2, 3, plane, 2 * zone_z), f32),
            pltpu.VMEM((3, 2 * pad_x, 2 * zone_z), f32),
            pltpu.VMEM((wide, lanes), f32),
            pltpu.VMEM((3 * MATS + 8, tile, 2 * zone_z), f32),
            pltpu.VMEM((3, wide, 3 * lanes), f32),
            pltpu.VMEM((3, wide, 3 * lanes), f32),
            pltpu.VMEM((ROUNDS, 3, plane, 2 * zone_z), f32),
            pltpu.VMEM((ROUNDS, 2, node_x, 3, 1, 2 * zone_z), f32),
            pltpu.VMEM((ROUNDS, 4, 3, 1, 2 * zone_z), f32),
            pltpu.VMEM((ROUNDS, 2, 3, pad_y, 2 * zone_z), f32),
            pltpu.VMEM((ROUNDS, 2, node_x, 3, 1, 2 * zone_z), f32),
            pltpu.VMEM((ROUNDS, 4, 3, 1, 2 * zone_z), f32),
            pltpu.VMEM((n_dom, 8, 2 * zone_z), f32),
            pltpu.VMEM((n_sub, 8, 2 * zone_z), f32),
            pltpu.SemaphoreType.DMA((ROUNDS, 8)),
            pltpu.SemaphoreType.DMA((ROUNDS, 8)),
            pltpu.SemaphoreType.DMA((n_dom,)),
            pltpu.SemaphoreType.DMA((n_dom,)),
            pltpu.SemaphoreType.DMA((n_sub,)),
            pltpu.SemaphoreType.DMA((n_sub,)),
        ],
        compiler_params=pltpu.CompilerParams(
            collective_id=0, has_side_effects=True, vmem_limit_bytes=48 * 2**20
        ),
    )(*inputs)
    hbm = pl.BlockSpec(memory_space=pltpu.HBM)
    accel, residual, energy_rate = pl.pallas_call(
        functools.partial(combine_kernel, node_y, pad_y),
        out_shape=(nodes_out, nodes_out, rate_out),
        in_specs=[vmem] * 3,
        out_specs=(hbm,) * 3,
        scratch_shapes=[
            pltpu.VMEM(nodes_out.shape, f32),
            pltpu.VMEM(nodes_out.shape, f32),
            pltpu.SemaphoreType.DMA((3,)),
        ],
        compiler_params=pltpu.CompilerParams(vmem_limit_bytes=8 * 2**20),
    )(total, factors, rate)
    back = (2, 0, 1, 3)
    return jnp.transpose(accel, back), jnp.transpose(residual, back), energy_rate


def solution(mesh):
    blocks = P(None, "dom", "sub", None)
    return jax.shard_map(
        per_device,
        mesh=mesh,
        in_specs=(blocks,) * 6 + (P("dom", "sub", None), blocks),
        out_specs=(blocks,) * 3,
        check_vma=False,
    )
```

```python
import functools
import math

import jax
import jax.numpy as jnp
import numpy as np
from jax import lax
from jax.experimental import pallas as pl
from jax.experimental.pallas import tpu as pltpu
from jax.sharding import PartitionSpec as P
import ml_dtypes

MESH = pl.DeviceIdType.MESH
MATS = 4
EQ_ITERS = 4
CG_ITERS = 3
ROUNDS = CG_ITERS + 1
N_INPUTS = 18

gammas = (1.4, 1.67, 2.0, 3.0)
cold_terms = (0.3, 1.2, 0.6, 2.4)

spread_root = math.sqrt(0.15)
points = np.array([0.5 - spread_root, 0.5, 0.5 + spread_root])
quad_one = np.array([5.0, 8.0, 5.0]) / 18.0
value_one = np.stack(
    [
        2.0 * (points - 0.5) * (points - 1.0),
        -4.0 * points * (points - 1.0),
        2.0 * points * (points - 0.5),
    ],
    1,
)
slope_one = np.stack([4.0 * points - 3.0, 4.0 - 8.0 * points, 4.0 * points - 1.0], 1)
linear_one = np.stack([1.0 - points, points], 1)


def round_up(value, step):
    return -(-value // step) * step


def split_table(table, axis):
    table = table.astype(np.float32)
    high = table.astype(ml_dtypes.bfloat16)
    low = (table - high.astype(np.float32)).astype(ml_dtypes.bfloat16)
    return np.concatenate([high, high, low], axis)


def depth_matrix(one, zone_z, lanes):
    table = np.zeros((2 * zone_z, lanes))
    for q in range(3):
        for z in range(zone_z):
            for k in range(3):
                table[(2 * z + k) % (2 * zone_z), q * zone_z + z] += one[q, k]
    return table


def plane_matrix(one_x, one_y, zone_x, zone_y, pad_y):
    table = np.zeros((9 * zone_x * zone_y, (2 * zone_x + 1) * pad_y))
    for a in range(3):
        for b in range(3):
            for x in range(zone_x):
                for y in range(zone_y):
                    row = ((a * 3 + b) * zone_x + x) * zone_y + y
                    for i in range(3):
                        for j in range(3):
                            table[row, (2 * x + i) * pad_y + 2 * y + j] = one_x[a, i] * one_y[b, j]
    return table


def split_lanes(x):
    high = x.astype(jnp.bfloat16)
    low = (x - high.astype(jnp.float32)).astype(jnp.bfloat16)
    return jnp.concatenate([high, low, high], axis=1)


def split_rows(x):
    high = x.astype(jnp.bfloat16).astype(jnp.float32)
    return jnp.concatenate([high, x - high, high], axis=0).astype(jnp.bfloat16)


def product(left, right):
    return jnp.dot(left, right, preferred_element_type=jnp.float32)


def lanes_of(x, rows):
    return jnp.concatenate([x[c * rows : (c + 1) * rows] for c in range(3)], axis=1)


def rows_of(x, lanes):
    return jnp.concatenate([x[:, c * lanes : (c + 1) * lanes] for c in range(3)], axis=0)


def kernel(
    dims,
    *refs,
):
    outer, refs = refs[:N_INPUTS], refs[N_INPUTS:]
    outputs, refs = refs[:3], refs[3:]
    inner, refs = refs[:N_INPUTS], refs[N_INPUTS:]
    body(dims, outer, *inner, *outputs, *refs)


def body(
    dims,
    outer,
    displacement,
    depth_value,
    depth_slope,
    plane_slopes,
    plane_value,
    material_id,
    mix_mask,
    mass_share,
    energy_share,
    energy,
    rho_weight,
    weight_table,
    plane_slopes_t,
    plane_value_t,
    depth_both_t,
    velocity,
    depth_value_t,
    plane_sides,
    total,
    factors,
    energy_rate,
    load_sem,
    field,
    rows_y,
    rho,
    zone_in,
    jac,
    stress,
    part,
    side_y,
    side_corner,
    face_x,
    face_y,
    corner,
    dom_parts,
    sub_parts,
    halo_send,
    halo_recv,
    dom_send,
    dom_recv,
    sub_send,
    sub_recv,
):
    n_dom, n_sub, zone_x, zone_y, zone_z, pad_x, pad_y, lanes = dims
    node_x, node_y = 2 * zone_x + 1, 2 * zone_y + 1
    plane = node_x * pad_y
    tile = zone_x * zone_y
    wide = 9 * tile
    me_dom, me_sub = lax.axis_index("dom"), lax.axis_index("sub")

    def at(shift_dom, shift_sub):
        return (lax.rem(me_dom + shift_dom + n_dom, n_dom), lax.rem(me_sub + shift_sub + n_sub, n_sub))

    corners = [(-1, -1), (-1, 1), (1, -1), (1, 1)]
    along_dom = [at(k, 0) for k in range(1, n_dom)]
    along_sub = [at(0, k) for k in range(1, n_sub)]
    diagonal = [at(dx, dy) for dx, dy in corners]
    beside_x, beside_y = (along_dom[-1], along_dom[0]), (along_sub[-1], along_sub[0])
    others = along_dom + along_sub + diagonal

    def gradients(which):
        source = split_lanes(field[which].reshape(3 * plane, 2 * zone_z))
        by_value = split_rows(lanes_of(product(source, depth_value[...]), plane))
        by_slope = split_rows(lanes_of(product(source, depth_slope[...]), plane))
        along_xy = product(plane_slopes[...], by_value)
        along_z = product(plane_value[...], by_slope)
        jac[0] = along_xy[:wide]
        jac[1] = along_xy[wide:]
        jac[2] = along_z

    inner = (
        displacement, depth_value, depth_slope, plane_slopes, plane_value, material_id, mix_mask,
        mass_share, energy_share, energy, rho_weight, weight_table, plane_slopes_t, plane_value_t,
        depth_both_t, velocity, depth_value_t, plane_sides,
    )
    loads = [pltpu.make_async_copy(a, b, load_sem.at[k]) for k, (a, b) in enumerate(zip(outer, inner))]
    for load in loads:
        load.start()
    barrier = pltpu.get_barrier_semaphore()
    for other in others:
        pl.semaphore_signal(barrier, inc=1, device_id=other, device_id_type=MESH)
    field[...] = jnp.zeros_like(field)
    rows_y[...] = jnp.zeros_like(rows_y)

    def unpack(which, source):
        for x in range(node_x):
            for c in range(3):
                field[which, c, x * pad_y : x * pad_y + node_y, :] = source[x, :, c, :]

    loads[0].wait()
    unpack(0, displacement)
    for load in loads[1:5]:
        load.wait()
    gradients(0)
    for load in loads[5:]:
        load.wait()
    for t in range(9):
        for q in range(4):
            for x in range(zone_x):
                rho[t * tile + x * zone_y : t * tile + (x + 1) * zone_y, q * zone_z : (q + 1) * zone_z] = (
                    rho_weight[3 * t + q % 3, x]
                )
    for half in range(2):
        cols = slice(half * zone_z, (half + 1) * zone_z)
        for x in range(zone_x):
            rows = slice(x * zone_y, (x + 1) * zone_y)
            for m in range(MATS):
                present = jnp.where((mix_mask[m, x] == 1) | (material_id[x] == m), 1.0, 0.0)
                zone_in[m, rows, cols] = present
                zone_in[MATS + m, rows, cols] = mass_share[m, x]
                zone_in[2 * MATS + m, rows, cols] = energy_share[m, x]
            for j in range(8):
                zone_in[3 * MATS + j, rows, cols] = energy[j, x]

    present = [zone_in[m] for m in range(MATS)]
    weighted = [present[m] * zone_in[MATS + m] for m in range(MATS)]
    weighted_sum = 1.0 / (weighted[0] + weighted[1] + weighted[2] + weighted[3])
    present_sum = 1.0 / (present[0] + present[1] + present[2] + present[3])

    def spread(x):
        return jnp.concatenate([jnp.concatenate([x, x], axis=1)] * 3, axis=0)

    start = [spread(present[m] * present_sum) for m in range(MATS)]
    load = [
        spread((gammas[m] - 1.0) * (weighted[m] * weighted_sum) * zone_in[2 * MATS + m])
        for m in range(MATS)
    ]
    lane_at = lax.broadcasted_iota(jnp.int32, (tile, lanes), 1) // zone_z
    upper = jnp.where(lane_at == 1, points[1], jnp.where(lane_at == 2, points[2], points[0])).astype(
        jnp.float32
    )
    along = []
    for j in range(4):
        low, high = zone_in[3 * MATS + 2 * j], zone_in[3 * MATS + 2 * j + 1]
        low, high = jnp.concatenate([low, low], axis=1), jnp.concatenate([high, high], axis=1)
        along.append(low + upper * (high - low))

    for a in range(3):
        rows = slice(a * 3 * tile, (a + 1) * 3 * tile)
        x_low = [linear_one[a, 0] * along[jy] + linear_one[a, 1] * along[2 + jy] for jy in range(2)]
        energy_points = jnp.concatenate(
            [linear_one[b, 0] * x_low[0] + linear_one[b, 1] * x_low[1] for b in range(3)], axis=0
        )

        def entry(c, d):
            value = jac[d, rows, c * lanes : (c + 1) * lanes]
            return value + 1.0 if c == d else value

        matrix = [[entry(c, d) for d in range(3)] for c in range(3)]
        adjugate = [[None] * 3 for _ in range(3)]
        for d in range(3):
            for c in range(3):
                adjugate[d][c] = (
                    matrix[(c + 1) % 3][(d + 1) % 3] * matrix[(c + 2) % 3][(d + 2) % 3]
                    - matrix[(c + 1) % 3][(d + 2) % 3] * matrix[(c + 2) % 3][(d + 1) % 3]
                )
        determinant = (
            matrix[0][0] * adjugate[0][0]
            + matrix[0][1] * adjugate[1][0]
            + matrix[0][2] * adjugate[2][0]
        )
        base = rho[rows, :] / determinant * energy_points
        pressure_load = [load[m] * base for m in range(MATS)]
        fraction = list(start)
        for sweep in range(EQ_ITERS):
            grown = []
            for m in range(MATS):
                square = fraction[m] * (pressure_load[m] + cold_terms[m] * fraction[m])
                grown.append(square * lax.rsqrt(jnp.maximum(square, 1e-30)))
            scale = 1.0 / ((grown[0] + grown[1]) + (grown[2] + grown[3]))
            fraction = [grown[m] * scale for m in range(MATS)]
        pressure = (
            (pressure_load[0] + cold_terms[0] * fraction[0])
            + (pressure_load[1] + cold_terms[1] * fraction[1])
            + (pressure_load[2] + cold_terms[2] * fraction[2])
            + (pressure_load[3] + cold_terms[3] * fraction[3])
        )
        weighted_pressure = weight_table[rows, :] * pressure
        for d in range(3):
            for c in range(3):
                stress[d, rows, c * lanes : (c + 1) * lanes] = weighted_pressure * adjugate[d][c]

    sends = []

    def send(source, target, to, send_sem, recv_sem):
        copy = pltpu.make_async_remote_copy(
            src_ref=source,
            dst_ref=target,
            send_sem=send_sem,
            recv_sem=recv_sem,
            device_id=to,
            device_id_type=MESH,
        )
        copy.start()
        sends.append(copy)
        return copy

    last = node_x - 1

    def start_halo(turn):
        for k in range(2):
            row = k * (node_y - 1)
            for x in range(node_x):
                for c in range(3):
                    line = part[turn, c, x * pad_y + row : x * pad_y + row + 1, :]
                    side_y[turn, k, x, c] = line
                    if x == 0:
                        side_corner[turn, k, c] = line
                    if x == last:
                        side_corner[turn, 2 + k, c] = line
        copies = []
        for k, (dx, dy) in enumerate(corners):
            copies.append(
                send(
                    side_corner.at[turn, k],
                    corner.at[turn, k],
                    diagonal[k],
                    halo_send.at[turn, 4 + k],
                    halo_recv.at[turn, 4 + k],
                )
            )
        for k, dy in enumerate((-1, 1)):
            copies.append(
                send(
                    side_y.at[turn, k],
                    face_y.at[turn, k],
                    beside_y[k],
                    halo_send.at[turn, 2 + k],
                    halo_recv.at[turn, 2 + k],
                )
            )
        for k, dx in enumerate((-1, 1)):
            first = 0 if dx < 0 else last * pad_y
            copies.append(
                send(
                    part.at[turn, :, pl.ds(first, pad_y), :],
                    face_x.at[turn, k],
                    beside_x[k],
                    halo_send.at[turn, k],
                    halo_recv.at[turn, k],
                )
            )
        return copies

    def finish_x(turn, copies):
        for copy in copies[6:]:
            copy.wait_recv()
        for x in range(node_x):
            block = part[turn, :, x * pad_y : (x + 1) * pad_y, :]
            if x == 0:
                block = block + face_x[turn, 1]
            if x == last:
                block = block + face_x[turn, 0]
            total[turn, :, x * pad_y : (x + 1) * pad_y, :] = block

    def finish_y(turn, copies):
        for copy in copies[:6]:
            copy.wait_recv()
        for x in range(node_x):
            for c in range(3):
                for k in range(2):
                    line = face_y[turn, 1 - k, x, c]
                    if x == 0:
                        line = line + corner[turn, 3 - k, c]
                    if x == last:
                        line = line + corner[turn, 1 - k, c]
                    rows_y[c, k * pad_x + x : k * pad_x + x + 1, :] = line

    def add_y(turn):
        for x in range(node_x):
            for k in range(2):
                row = x * pad_y + k * (node_y - 1)
                total[turn, :, row : row + 1, :] += rows_y[:, k * pad_x + x : k * pad_x + x + 1, :]

    def owned(turn):
        return [
            total[turn, c, x * pad_y : x * pad_y + 2 * zone_y, :]
            for c in range(3)
            for x in range(2 * zone_x)
        ]

    def tree(terms):
        while len(terms) > 1:
            terms = [sum(terms[k : k + 2]) for k in range(0, len(terms), 2)]
        return jnp.sum(terms[0], axis=0, keepdims=True)

    def square(turn):
        return tree([a * a for a in owned(turn)])

    def energy_of(at_points, scaled):
        both = at_points * scaled
        return tree(
            [
                both[t * tile : (t + 1) * tile, k * 2 * zone_z : (k + 1) * 2 * zone_z]
                for t in range(9)
                for k in range(3 * lanes // (2 * zone_z))
            ]
        )

    side_xy = product(
        plane_slopes_t[...],
        split_rows(jnp.concatenate([stress[0], stress[1]], axis=0)),
    )
    side_z = product(plane_value_t[...], split_rows(stress[2]))
    both = jnp.concatenate([rows_of(side_xy, lanes), rows_of(side_z, lanes)], axis=1)
    part[0] = product(split_lanes(both), depth_both_t[...]).reshape(3, plane, 2 * zone_z)
    pl.semaphore_wait(barrier, len(others))
    copies = start_halo(0)

    mass_weight = weight_table[...] * rho[...]

    def contract():
        work = jnp.zeros((wide, lanes), jnp.float32)
        for c in range(3):
            for d in range(3):
                cols = slice(c * lanes, (c + 1) * lanes)
                work = work + jac[d, :, cols] * stress[d, :, cols]
        return work

    def to_linear(x):
        results = []
        for jx in range(2):
            for jy in range(2):
                acc = jnp.zeros((tile, lanes), jnp.float32)
                for a in range(3):
                    for b in range(3):
                        t = a * 3 + b
                        acc = acc + float(linear_one[a, jx] * linear_one[b, jy]) * x[t * tile : (t + 1) * tile]
                for jz in range(2):
                    scaled = acc * (upper if jz else 1.0 - upper)
                    folded = scaled[:, : 2 * zone_z] + scaled[:, 2 * zone_z :]
                    results.append(folded + pltpu.roll(folded, zone_z, 1))
        return results

    def store_rate():
        rates = to_linear(contract())
        lumped = to_linear(mass_weight)
        for j in range(8):
            rate = -rates[j] / lumped[j]
            for x in range(zone_x):
                energy_rate[j, x] = rate[x * zone_y : (x + 1) * zone_y, :zone_z]

    moments = []
    weight_three = jnp.concatenate([mass_weight] * 3, axis=1)
    for turn in range(1, ROUNDS):
        finish_x(turn - 1, copies)
        source = split_lanes(total[turn - 1].reshape(3 * plane, 2 * zone_z))
        nodes = split_rows(lanes_of(product(source, depth_value[...]), plane))
        at_points = product(plane_value[...], nodes)
        finish_y(turn - 1, copies)
        source = split_lanes(rows_y[...].reshape(6 * pad_x, 2 * zone_z))
        nodes = split_rows(lanes_of(product(source, depth_value[...]), 2 * pad_x))
        at_points = at_points + product(plane_sides[...], nodes)
        scaled = at_points * weight_three
        if turn == ROUNDS - 1:
            add_y(turn - 1)
            moments += [square(turn - 1), energy_of(at_points, scaled)]
            fill = jnp.zeros((8 - len(moments), 2 * zone_z), jnp.float32)
            dom_parts[0] = jnp.concatenate(moments + [fill], axis=0)
            dom_copies = [
                send(dom_parts.at[0], dom_parts.at[k], along_dom[k - 1], dom_send.at[k], dom_recv.at[k])
                for k in range(1, n_dom)
            ]
        back = product(plane_value_t[...], split_rows(scaled))
        part[turn] = product(split_lanes(rows_of(back, lanes)), depth_value_t[...]).reshape(
            3, plane, 2 * zone_z
        )
        copies = start_halo(turn)
        if turn < ROUNDS - 1:
            add_y(turn - 1)
            moments += [square(turn - 1), energy_of(at_points, scaled)]
        if turn == 1:
            unpack(1, velocity)
            gradients(1)
        if turn == 2:
            store_rate()
    for copy in dom_copies:
        copy.wait_recv()
    sub_parts[0] = jnp.sum(dom_parts[...], axis=0)
    sub_copies = [
        send(sub_parts.at[0], sub_parts.at[k], along_sub[k - 1], sub_send.at[k], sub_recv.at[k])
        for k in range(1, n_sub)
    ]
    finish_x(ROUNDS - 1, copies)
    finish_y(ROUNDS - 1, copies)
    add_y(ROUNDS - 1)
    for copy in sub_copies:
        copy.wait_recv()
    summed = jnp.sum(jnp.sum(sub_parts[...], axis=0), axis=1, keepdims=True)
    mom = [jnp.broadcast_to(summed[k : k + 1], (1, 2 * zone_z)) for k in range(2 * CG_ITERS)]

    def inner(left, right, shift):
        acc = None
        for i, a in enumerate(left):
            for j, b in enumerate(right):
                term = a * b * mom[i + j + shift]
                acc = term if acc is None else acc + term
        return acc

    def combine(left, right, factor):
        out = []
        for k in range(max(len(left), len(right))):
            if k >= len(right):
                out.append(left[k])
            elif k >= len(left):
                out.append(factor * right[k])
            else:
                out.append(left[k] + factor * right[k])
        return out

    one = jnp.ones((1, 2 * zone_z), jnp.float32)
    nil = jnp.zeros((1, 2 * zone_z), jnp.float32)
    answer, rest, direction = [], [one], [one]
    norm = mom[0]
    for sweep in range(CG_ITERS):
        step = norm / inner(direction, direction, 1)
        answer = combine(answer, direction, step)
        rest = combine(rest, [nil] + direction, -step)
        if sweep + 1 < CG_ITERS:
            norm_next = inner(rest, rest, 0)
            direction = combine(rest, direction, norm_next / norm)
            norm = norm_next
    for k, factor in enumerate(answer + rest):
        factors[k] = factor
    for copy in sends:
        copy.wait_send()


def combine_kernel(node_y, pad_y, total, factors, rate, accel, residual, energy_rate, one, two, sem):
    rate_copy = pltpu.make_async_copy(rate, energy_rate, sem.at[0])
    rate_copy.start()
    for k, (spot, out, first, count) in enumerate(
        ((one, accel, 0, CG_ITERS), (two, residual, CG_ITERS, ROUNDS))
    ):
        for x in range(one.shape[0]):
            for c in range(3):
                terms = [
                    factors[first + i] * total[i, c, x * pad_y : x * pad_y + node_y, :]
                    for i in range(count)
                ]
                spot[x, :, c, :] = sum(terms[1:], terms[0])
        pltpu.make_async_copy(spot, out, sem.at[1 + k]).start()
    rate_copy.wait()
    for k, (spot, out) in enumerate(((one, accel), (two, residual))):
        pltpu.make_async_copy(spot, out, sem.at[1 + k]).wait()


def per_device(
    velocity, displacement, energy, rho_weight, mass_share, energy_share, material_id, mix_mask
):
    n_dom, n_sub = lax.axis_size("dom"), lax.axis_size("sub")
    zone_x, zone_y, zone_z = energy.shape[1:]
    node_x, node_y = 2 * zone_x + 1, 2 * zone_y + 1
    pad_x, pad_y = round_up(node_x, 8), round_up(node_y, 8)
    lanes = 4 * zone_z
    plane, wide, tile = node_x * pad_y, 9 * zone_x * zone_y, zone_x * zone_y
    dims = (n_dom, n_sub, zone_x, zone_y, zone_z, pad_x, pad_y, lanes)

    z_value = depth_matrix(value_one, zone_z, lanes)
    z_slope = depth_matrix(slope_one, zone_z, lanes)
    xy = [
        plane_matrix(first, second, zone_x, zone_y, pad_y)
        for first, second in ((value_one, value_one), (slope_one, value_one), (value_one, slope_one))
    ]
    xy_t = [table.T for table in xy]
    sides = np.zeros((wide, 2 * pad_x))
    for x in range(node_x):
        sides[:, x] = xy[0][:, x * pad_y]
        sides[:, pad_x + x] = xy[0][:, x * pad_y + 2 * zone_y]
    weights = np.zeros((9, tile, 4, zone_z), np.float32)
    for a in range(3):
        for b in range(3):
            for q in range(3):
                weights[a * 3 + b, :, q] = quad_one[a] * quad_one[b] * quad_one[q]
    order = (1, 2, 0, 3)
    inputs = (
        jnp.transpose(displacement, order),
        split_table(z_value, 0),
        split_table(z_slope, 0),
        split_table(np.concatenate([xy[1], xy[2]], 0), 1),
        split_table(xy[0], 1),
        material_id,
        mix_mask,
        mass_share,
        energy_share,
        energy,
        rho_weight,
        weights.reshape(wide, lanes),
        split_table(np.concatenate([xy_t[1], xy_t[2]], 1), 1),
        split_table(xy_t[0], 1),
        split_table(np.concatenate([z_value.T, z_slope.T], 0), 0),
        jnp.transpose(velocity, order),
        split_table(z_value.T, 0),
        split_table(sides, 1),
    )
    inputs = [pltpu.with_memory_space_constraint(jnp.asarray(array), pltpu.HBM) for array in inputs]
    f32 = jnp.float32
    vmem = pl.BlockSpec(memory_space=pltpu.VMEM)
    nodes_out = jax.ShapeDtypeStruct((node_x, node_y, 3, 2 * zone_z), f32)
    rate_out = jax.ShapeDtypeStruct(energy.shape, f32)
    total, factors, rate = pl.pallas_call(
        functools.partial(kernel, dims),
        out_shape=(
            jax.ShapeDtypeStruct((ROUNDS, 3, plane, 2 * zone_z), f32),
            jax.ShapeDtypeStruct((CG_ITERS + ROUNDS, 1, 2 * zone_z), f32),
            rate_out,
        ),
        in_specs=[pl.BlockSpec(memory_space=pltpu.HBM)] * N_INPUTS,
        out_specs=(vmem,) * 3,
        scratch_shapes=[pltpu.VMEM(array.shape, array.dtype) for array in inputs]
        + [
            pltpu.SemaphoreType.DMA((N_INPUTS,)),
            pltpu.VMEM((2, 3, plane, 2 * zone_z), f32),
            pltpu.VMEM((3, 2 * pad_x, 2 * zone_z), f32),
            pltpu.VMEM((wide, lanes), f32),
            pltpu.VMEM((3 * MATS + 8, tile, 2 * zone_z), f32),
            pltpu.VMEM((3, wide, 3 * lanes), f32),
            pltpu.VMEM((3, wide, 3 * lanes), f32),
            pltpu.VMEM((ROUNDS, 3, plane, 2 * zone_z), f32),
            pltpu.VMEM((ROUNDS, 2, node_x, 3, 1, 2 * zone_z), f32),
            pltpu.VMEM((ROUNDS, 4, 3, 1, 2 * zone_z), f32),
            pltpu.VMEM((ROUNDS, 2, 3, pad_y, 2 * zone_z), f32),
            pltpu.VMEM((ROUNDS, 2, node_x, 3, 1, 2 * zone_z), f32),
            pltpu.VMEM((ROUNDS, 4, 3, 1, 2 * zone_z), f32),
            pltpu.VMEM((n_dom, 8, 2 * zone_z), f32),
            pltpu.VMEM((n_sub, 8, 2 * zone_z), f32),
            pltpu.SemaphoreType.DMA((ROUNDS, 8)),
            pltpu.SemaphoreType.DMA((ROUNDS, 8)),
            pltpu.SemaphoreType.DMA((n_dom,)),
            pltpu.SemaphoreType.DMA((n_dom,)),
            pltpu.SemaphoreType.DMA((n_sub,)),
            pltpu.SemaphoreType.DMA((n_sub,)),
        ],
        compiler_params=pltpu.CompilerParams(
            collective_id=0, has_side_effects=True, vmem_limit_bytes=48 * 2**20
        ),
    )(*inputs)
    hbm = pl.BlockSpec(memory_space=pltpu.HBM)
    accel, residual, energy_rate = pl.pallas_call(
        functools.partial(combine_kernel, node_y, pad_y),
        out_shape=(nodes_out, nodes_out, rate_out),
        in_specs=[vmem] * 3,
        out_specs=(hbm,) * 3,
        scratch_shapes=[
            pltpu.VMEM(nodes_out.shape, f32),
            pltpu.VMEM(nodes_out.shape, f32),
            pltpu.SemaphoreType.DMA((3,)),
        ],
        compiler_params=pltpu.CompilerParams(vmem_limit_bytes=8 * 2**20),
    )(total, factors, rate)
    back = (2, 0, 1, 3)
    return jnp.transpose(accel, back), jnp.transpose(residual, back), energy_rate


def solution(mesh):
    blocks = P(None, "dom", "sub", None)
    return jax.shard_map(
        per_device,
        mesh=mesh,
        in_specs=(blocks,) * 6 + (P("dom", "sub", None), blocks),
        out_specs=(blocks,) * 3,
        check_vma=False,
    )
```
